32 devices in a mesh: tm: 4 (over y, core), asset: 8 (over z, x).
Axes of the slice: x: 2, y: 2, z: 4, core: 2. Of those that a mesh axis runs over, the one named last changes fastest.
Arguments:
- features: bfloat16 [8, 10240, 512], P('tm', 'asset'), may hold values from -6 to 6
- w_value: bfloat16 [512, 512], replicated, may hold values from -0.25 to 0.25
- w_gate: bfloat16 [512, 512], replicated, may hold values from -0.25 to 0.25
- cotangent: bfloat16 [8, 10240, 512], P('tm', 'asset'), may hold values from -6 to 6
- local_rows: int32 [160], P('asset'), may hold values from 0 to 9
- local_cols: int32 [160], P('asset'), may hold values from 0 to 9
- local_count: int32 [8], P('asset'), may hold values from 10 to 20, as said below
- local_tiles: bfloat16 [160, 128, 128], P('asset'), may hold values from -0.3125 to 0.3125
- remote_rows: int32 [64], P('asset'), may hold values from 0 to 9
- remote_cols: int32 [64], P('asset'), may hold values from 0 to 9
- remote_live: int32 [64], P('asset'), may hold values from 0 to 1, as said below
- remote_tiles: bfloat16 [64, 128, 128], P('asset'), may hold values from -0.3125 to 0.3125
Outputs:
- output: bfloat16 [8, 10240, 512], P('tm', 'asset')
- grad_features: bfloat16 [8, 10240, 512], P('tm', 'asset')
- grad_value: float32 [512, 512], replicated
- grad_gate: float32 [512, 512], replicated
The draws below stay inside these ranges and needn't reach their ends.
Inputs may be any that keep to these rules, and one draw needn't show every extreme that they name: `local_count`: used local slots of each index of asset; some index uses all 20 in every draw. `remote_live`: at most one remote tile for each pair of indices of asset, never from an index to itself; in every draw some index holds a tile for every other index, and some index receives a tile from every other index.
All inputs are finite; a program needn't handle non-finite values.
Results may differ from the reference program's by a relative error of at most 0.0057.
Values may be sent and summed in bfloat16 or wider, within the bound.
No kernel may reach another device: no remote copies, remote signals or barrier semaphores. Data moves between devices by JAX's collectives and lax.ppermute only.
A program may use at most 128 MiB of HBM per device.

```python
import jax
import jax.numpy as jnp
from jax import lax

D = 512
TILE = 128
BLK_DEV = 10
LOC = 20
ASSETS = 10240
TIME = 8
N_ASSET = 8


def draw_local_count(key, part):
    key_base = jax.random.fold_in(key, 11)
    first, second = jax.random.split(key_base)
    counts = jax.random.randint(first, (N_ASSET,), BLK_DEV, LOC + 1)
    chosen = jax.random.randint(second, (), 0, N_ASSET)
    return jnp.where(jnp.arange(N_ASSET) == chosen, LOC, counts).astype(jnp.int32)


def draw_remote_live(key, part):
    key_base = jax.random.fold_in(key, 23)
    first, second, third = jax.random.split(key_base, 3)
    live = (jax.random.randint(first, (N_ASSET, N_ASSET), 0, 5) < 3).astype(jnp.int32)
    sender = jax.random.randint(second, (), 0, N_ASSET)
    receiver = jax.random.randint(third, (), 0, N_ASSET)
    source = jnp.arange(N_ASSET)[:, None]
    target = jnp.arange(N_ASSET)[None, :]
    live = jnp.where(source == sender, 1, live)
    live = jnp.where(target == receiver, 1, live)
    live = jnp.where(source == target, 0, live)
    return live.reshape(-1).astype(jnp.int32)


def touch_ends(result, own_key, least, high):
    index_at = [jax.random.randint(jax.random.fold_in(own_key, axis), (), 0, length) for axis, length in enumerate(result.shape)]
    widest = result.shape.index(max(result.shape))
    beside = index_at[:widest] + [(index_at[widest] + 1) % result.shape[widest]] + index_at[widest + 1:]
    return result.at[tuple(index_at)].set(least).at[tuple(beside)].set(high)


def block_levels(stream_key, dims, pieces, low, top_value):
    loudness, own = 1.0, jax.random.fold_in(stream_key, 6)
    for dim, parts in pieces:
        draws = jnp.exp(jax.random.uniform(jax.random.fold_in(own, dim), (parts,), jnp.float32, low / len(pieces), top_value / len(pieces)))
        loudness = loudness * jnp.repeat(draws, dims[dim] // parts).reshape([-1 if axis == dim else 1 for axis in range(len(dims))])
    return loudness


def noise(key, extent, scale, limit, shards=(), kind=jnp.bfloat16):
    level = block_levels(key, extent, shards, -0.22, 0.18) if shards else 1.0
    result = jax.random.normal(key, extent, jnp.float32) * scale * level
    return jnp.minimum(jnp.maximum(result, -limit), limit).astype(kind)


def setup_inputs(seed: int = 0) -> dict:
    splits = jax.random.split(jax.random.key(seed), 13)
    features = noise(splits[0], (TIME, ASSETS, D), 1.0, 6.0, ((0, 4), (1, 8)))
    w_value = noise(splits[1], (D, D), D ** -0.5, 0.25)
    w_gate = noise(splits[2], (D, D), D ** -0.5, 0.25)
    cotangent = noise(splits[3], (TIME, ASSETS, D), 1.0, 6.0, ((0, 4), (1, 8)))
    local_rows = touch_ends(jax.random.randint(splits[4], (N_ASSET * LOC,), 0, BLK_DEV), jax.random.fold_in(splits[4], 1), 0, BLK_DEV - 1).astype(jnp.int32)
    local_cols = touch_ends(jax.random.randint(splits[5], (N_ASSET * LOC,), 0, BLK_DEV), jax.random.fold_in(splits[5], 1), 0, BLK_DEV - 1).astype(jnp.int32)
    local_count = draw_local_count(jax.random.fold_in(splits[12], 71), 0)
    local_tiles = noise(splits[7], (N_ASSET * LOC, TILE, TILE), (3 * TILE) ** -0.5, 0.3125, ((0, 8),))
    remote_rows = touch_ends(jax.random.randint(splits[8], (N_ASSET * N_ASSET,), 0, BLK_DEV), jax.random.fold_in(splits[8], 1), 0, BLK_DEV - 1).astype(jnp.int32)
    remote_cols = touch_ends(jax.random.randint(splits[9], (N_ASSET * N_ASSET,), 0, BLK_DEV), jax.random.fold_in(splits[9], 1), 0, BLK_DEV - 1).astype(jnp.int32)
    remote_live = draw_remote_live(jax.random.fold_in(splits[12], 71), 0)
    remote_tiles = noise(splits[11], (N_ASSET * N_ASSET, TILE, TILE), (3 * TILE) ** -0.5, 0.3125, ((0, 8),))
    return dict(features=features, w_value=w_value, w_gate=w_gate, cotangent=cotangent, local_rows=local_rows, local_cols=local_cols, local_count=local_count, local_tiles=local_tiles, remote_rows=remote_rows, remote_cols=remote_cols, remote_live=remote_live, remote_tiles=remote_tiles)


def tile_lists(local_rows, local_cols, local_count, local_tiles, remote_rows, remote_cols, remote_live, remote_tiles):
    slot = jnp.arange(N_ASSET * LOC, dtype=jnp.int32)
    owner = slot // LOC
    lrow = owner * BLK_DEV + local_rows
    lcol = owner * BLK_DEV + local_cols
    lmask = (slot % LOC < local_count[owner]).astype(jnp.float32)
    entry = jnp.arange(N_ASSET * N_ASSET, dtype=jnp.int32)
    source = entry // N_ASSET
    target = entry % N_ASSET
    rrow = target * BLK_DEV + remote_rows[target * N_ASSET + source]
    rcol = source * BLK_DEV + remote_cols
    rmask = remote_live.astype(jnp.float32)
    rows = jnp.concatenate([lrow, rrow]).astype(jnp.int32)
    cols = jnp.concatenate([lcol, rcol]).astype(jnp.int32)
    masks = jnp.concatenate([lmask, rmask])
    tiles = jnp.concatenate([local_tiles, remote_tiles], axis=0)
    return rows, cols, masks, tiles


def reference(features, w_value, w_gate, cotangent, local_rows, local_cols, local_count, local_tiles, remote_rows, remote_cols, remote_live, remote_tiles):
    blocks_all = N_ASSET * BLK_DEV
    flat = features.reshape(-1, D)
    value = jnp.dot(flat, w_value, preferred_element_type=jnp.float32).astype(jnp.bfloat16)
    gate = jax.nn.sigmoid(jnp.dot(flat, w_gate, preferred_element_type=jnp.float32))
    value_blocks = value.reshape(TIME, blocks_all, TILE, D)
    rows, cols, masks, tiles = tile_lists(local_rows, local_cols, local_count, local_tiles, remote_rows, remote_cols, remote_live, remote_tiles)

    def forward_step(total, item):
        row, col, mask, tile = item
        block = lax.dynamic_index_in_dim(value_blocks, col, 1, keepdims=False)
        term = jnp.einsum("ij,tjd->tid", tile.astype(jnp.float32), block.astype(jnp.float32)).astype(jnp.bfloat16)
        old = lax.dynamic_index_in_dim(total, row, 1, keepdims=False)
        new = old + term.astype(jnp.float32) * mask
        return lax.dynamic_update_index_in_dim(total, new, row, 1), None

    start = jnp.zeros((TIME, blocks_all, TILE, D), jnp.float32)
    agg_blocks, _ = lax.scan(forward_step, start, (rows, cols, masks, tiles))
    agg = agg_blocks.reshape(-1, D)
    output = (flat.astype(jnp.float32) + gate * agg).astype(jnp.bfloat16)
    grad_out = cotangent.reshape(-1, D).astype(jnp.float32)
    dagg = (grad_out * gate).astype(jnp.bfloat16)
    dgate = (grad_out * agg * gate * (1.0 - gate)).astype(jnp.bfloat16)
    dagg_blocks = dagg.reshape(TIME, blocks_all, TILE, D)

    def backward_step(total, item):
        row, col, mask, tile = item
        block = lax.dynamic_index_in_dim(dagg_blocks, row, 1, keepdims=False)
        term = jnp.einsum("ji,tjd->tid", tile.astype(jnp.float32), block.astype(jnp.float32)).astype(jnp.bfloat16)
        old = lax.dynamic_index_in_dim(total, col, 1, keepdims=False)
        new = old + term.astype(jnp.float32) * mask
        return lax.dynamic_update_index_in_dim(total, new, col, 1), None

    dvalue_blocks, _ = lax.scan(backward_step, start, (rows, cols, masks, tiles))
    dvalue = dvalue_blocks.reshape(-1, D).astype(jnp.bfloat16)
    grad_features = grad_out + jnp.dot(dvalue, w_value.T, preferred_element_type=jnp.float32)
    grad_features = grad_features + jnp.dot(dgate, w_gate.T, preferred_element_type=jnp.float32)
    scale = (TIME * ASSETS) ** -0.5
    grad_value = jnp.dot(flat.T, dvalue, preferred_element_type=jnp.float32) * scale
    grad_gate = jnp.dot(flat.T, dgate, preferred_element_type=jnp.float32) * scale
    return (output.reshape(TIME, ASSETS, D), grad_features.astype(jnp.bfloat16).reshape(TIME, ASSETS, D), grad_value, grad_gate)
```

```python
import math

import jax
import jax.numpy as jnp
from jax import lax
from jax.experimental import pallas as pl
from jax.experimental.pallas import tpu as pltpu
from jax.sharding import PartitionSpec as P

F32 = jnp.float32
BF16 = jnp.bfloat16
ANY = pl.BlockSpec(memory_space=pl.ANY)
VMEM = pl.BlockSpec(memory_space=pltpu.VMEM)
SMEM = pl.BlockSpec(memory_space=pltpu.SMEM)
MIB = 1 << 20


def params(mib):
    return pltpu.CompilerParams(vmem_limit_bytes=mib * MIB)


def cost(flops, moved):
    return pl.CostEstimate(flops=int(flops), bytes_accessed=int(moved), transcendentals=0)


def mm(a, b):
    return lax.dot_general(a, b, (((1,), (0,)), ((), ())), preferred_element_type=F32)


def mm_tn(a, b):
    return lax.dot_general(a, b, (((0,), (0,)), ((), ())), preferred_element_type=F32)


def mm_nt(a, b):
    return lax.dot_general(a, b, (((1,), (1,)), ((), ())), preferred_element_type=F32)


def after(x, *others):
    return lax.optimization_barrier((x,) + others)[0]


def row_chunk(rows, most):
    return max(c for c in range(8, most + 1, 8) if rows % c == 0)


def target_of(index, shift, n):
    return index ^ shift if n & (n - 1) == 0 else (index + shift) % n


def source_of(index, shift, n):
    return index ^ shift if n & (n - 1) == 0 else (index + n - shift) % n


def exchange(block, shift, n):
    return lax.ppermute(block, "asset", [(i, target_of(i, shift, n)) for i in range(n)])


def send_forward(me, features, tiles, cols, live, shifts, n):
    steps, _, width = features.shape
    tile = tiles.shape[1]
    count = len(shifts)

    def body(me_ref, cols_ref, live_ref, tiles_ref, f_ref, *rest):
        outs, (buf, sem) = rest[:count], rest[count:]
        copies = []
        for j, shift in enumerate(shifts):
            col = cols_ref[target_of(me_ref[0], shift, n)]
            start = pl.multiple_of(col * tile, tile)
            copy = pltpu.make_async_copy(f_ref.at[:, pl.ds(start, tile), :], buf.at[j], sem.at[j])
            copy.start()
            copies.append(copy)
        for j, shift in enumerate(shifts):
            to = target_of(me_ref[0], shift, n)
            weights = tiles_ref[to] * live_ref[to].astype(F32).astype(BF16)
            copies[j].wait()
            for t in range(steps):
                outs[j][t] = mm(weights, buf[j, t]).astype(BF16)

    block = jax.ShapeDtypeStruct((steps, tile, width), BF16)
    size = steps * tile * width
    return pl.pallas_call(
        body,
        out_shape=[block] * count,
        in_specs=[SMEM, SMEM, SMEM, VMEM, ANY],
        out_specs=[VMEM] * count,
        scratch_shapes=[pltpu.VMEM((count, steps, tile, width), BF16), pltpu.SemaphoreType.DMA((count,))],
        compiler_params=params(32),
        cost_estimate=cost(2 * count * size * tile, 4 * count * size),
        name="send_forward",
    )(me, cols, live, tiles, features)


def send_backward(me, back, rows, shifts, n, tile):
    steps, _, width = back.shape
    count = len(shifts)

    def body(me_ref, rows_ref, r_ref, *rest):
        outs, sem = rest[:count], rest[count]
        copies = []
        for j, shift in enumerate(shifts):
            row = rows_ref[target_of(me_ref[0], shift, n)]
            start = pl.multiple_of(row * tile, tile)
            copy = pltpu.make_async_copy(r_ref.at[:, pl.ds(start, tile), :], outs[j], sem.at[j])
            copy.start()
            copies.append(copy)
        for copy in copies:
            copy.wait()

    block = jax.ShapeDtypeStruct((steps, tile, width), BF16)
    return pl.pallas_call(
        body,
        out_shape=[block] * count,
        in_specs=[SMEM, SMEM, ANY],
        out_specs=[ANY] * count,
        scratch_shapes=[pltpu.SemaphoreType.DMA((count,))],
        compiler_params=params(32),
        cost_estimate=cost(0, 4 * count * steps * tile * width),
        name="send_backward",
    )(me, rows, back)


def project(flat, grad, w_value, w_gate):
    rows, width = flat.shape
    chunk = row_chunk(rows, 640)

    def body(f_ref, c_ref, wv_ref, wg_ref, gate_ref, dagg_ref, back_ref):
        gate = jax.nn.sigmoid(mm(f_ref[...], wg_ref[...]))
        gate_ref[...] = gate
        dagg = (c_ref[...].astype(F32) * gate).astype(BF16)
        dagg_ref[...] = dagg
        back_ref[...] = mm_nt(dagg, wv_ref[...]).astype(BF16)

    line = pl.BlockSpec((chunk, width), lambda i: (i, 0))
    whole = pl.BlockSpec((width, width), lambda i: (0, 0))
    half = jax.ShapeDtypeStruct((rows, width), BF16)
    return pl.pallas_call(
        body,
        grid=(rows // chunk,),
        out_shape=[jax.ShapeDtypeStruct((rows, width), F32), half, half],
        in_specs=[line, line, whole, whole],
        out_specs=[line] * 3,
        compiler_params=params(32),
        cost_estimate=cost(4 * rows * width * width, 12 * rows * width),
        name="project",
    )(flat, grad, w_value, w_gate)


def local_sum(tiles, count, place, pick, source, base):
    steps, assets, width = source.shape
    slots, tile, _ = tiles.shape
    transposed = base is not None

    def body(count_ref, place_ref, pick_ref, tiles_ref, s_ref, *rest):
        out = rest[-1]
        out[...] = rest[0][...].astype(F32) if transposed else jnp.zeros(out.shape, F32)

        @pl.loop(0, count_ref[0])
        def _(l):
            to = pl.ds(pl.multiple_of(place_ref[l] * tile, tile), tile)
            at = pl.ds(pl.multiple_of(pick_ref[l] * tile, tile), tile)
            weights = tiles_ref[l]
            for t in range(steps):
                block = s_ref[t, at, :]
                out[t, to, :] += mm_tn(weights, block) if transposed else mm(weights, block)

    extra = [base] if transposed else []
    return pl.pallas_call(
        body,
        out_shape=jax.ShapeDtypeStruct(source.shape, F32),
        in_specs=[SMEM, SMEM, SMEM, VMEM, VMEM] + [VMEM] * len(extra),
        out_specs=VMEM,
        compiler_params=params(40),
        cost_estimate=cost(2 * slots * tile * steps * tile * width, 8 * steps * assets * width),
        name="local_back" if transposed else "local_forward",
    )(count, place, pick, tiles, source, *extra)


def gather_sum(me, local, arrived, rows, dagg, shifts, n, tile):
    steps, assets, width = local.shape
    blocks = assets // tile
    count = len(shifts)
    per = max(p for p in range(1, 6) if blocks % p == 0)

    def body(me_ref, rows_ref, l_ref, d_ref, *rest):
        parts, (g_ref, w_ref) = rest[:count], rest[count:]
        t, b = pl.program_id(0), pl.program_id(1)
        g_ref[...] = l_ref[...]

        for j, shift in enumerate(shifts):
            place = rows_ref[source_of(me_ref[0], shift, n)] - b * per

            @pl.when((place >= 0) & (place < per))
            def _():
                to = pl.ds(pl.multiple_of(place * tile, tile), tile)
                g_ref[0, to, :] += parts[j][t].astype(F32)

        part = mm_tn(g_ref[0].astype(BF16), d_ref[0])

        @pl.when((t == 0) & (b == 0))
        def _():
            w_ref[...] = part

        @pl.when((t > 0) | (b > 0))
        def _():
            w_ref[...] += part

    line = pl.BlockSpec((1, per * tile, width), lambda t, b: (t, b, 0))
    piece = pl.BlockSpec((steps, tile, width), lambda t, b: (0, 0, 0))
    whole = pl.BlockSpec((width, width), lambda t, b: (0, 0))
    return pl.pallas_call(
        body,
        grid=(steps, blocks // per),
        out_shape=[jax.ShapeDtypeStruct(local.shape, F32), jax.ShapeDtypeStruct((width, width), F32)],
        in_specs=[SMEM, SMEM, line, line] + [piece] * count,
        out_specs=[line, whole],
        compiler_params=params(40),
        cost_estimate=cost(2 * steps * assets * width * width, 12 * steps * assets * width),
        name="gather_sum",
    )(me, rows, local, dagg, *arrived)


def mix(total, w_value, gate, flat, grad):
    rows, width = flat.shape
    chunk = row_chunk(rows, 640)

    def body(g_ref, wv_ref, gate_ref, f_ref, c_ref, out_ref, dgate_ref, w_ref):
        i = pl.program_id(0)
        agg = mm(g_ref[...].astype(BF16), wv_ref[...])
        gate = gate_ref[...]
        kept = gate * agg
        out_ref[...] = (f_ref[...].astype(F32) + kept).astype(BF16)
        dgate = (c_ref[...].astype(F32) * kept * (1.0 - gate)).astype(BF16)
        dgate_ref[...] = dgate
        part = mm_tn(f_ref[...], dgate)

        @pl.when(i == 0)
        def _():
            w_ref[...] = part

        @pl.when(i > 0)
        def _():
            w_ref[...] += part

    line = pl.BlockSpec((chunk, width), lambda i: (i, 0))
    whole = pl.BlockSpec((width, width), lambda i: (0, 0))
    half = jax.ShapeDtypeStruct((rows, width), BF16)
    return pl.pallas_call(
        body,
        grid=(rows // chunk,),
        out_shape=[half, half, jax.ShapeDtypeStruct((width, width), F32)],
        in_specs=[line, whole, line, line, line],
        out_specs=[line, line, whole],
        compiler_params=params(40),
        cost_estimate=cost(4 * rows * width * width, 16 * rows * width),
        name="mix",
    )(total, w_value, gate, flat, grad)


def add_gate(base, dgate, w_gate):
    rows, width = base.shape
    chunk = row_chunk(rows, 640)

    def body(b_ref, d_ref, w_ref, out_ref):
        out_ref[...] = b_ref[...] + mm_nt(d_ref[...], w_ref[...])

    line = pl.BlockSpec((chunk, width), lambda i: (i, 0))
    whole = pl.BlockSpec((width, width), lambda i: (0, 0))
    return pl.pallas_call(
        body,
        grid=(rows // chunk,),
        out_shape=jax.ShapeDtypeStruct((rows, width), F32),
        in_specs=[line, line, whole],
        out_specs=line,
        compiler_params=params(32),
        cost_estimate=cost(2 * rows * width * width, 10 * rows * width),
        name="add_gate",
    )(base, dgate, w_gate)


def finish(me, base, returned, cols, live, tiles, shifts, n):
    steps, assets, width = base.shape
    tile = tiles.shape[1]
    blocks = assets // tile
    count = len(shifts)

    def body(me_ref, cols_ref, live_ref, tiles_ref, b_ref, *rest):
        parts, (out_ref, acc) = rest[:count], rest[count:]
        b = pl.program_id(0)
        acc[...] = b_ref[...]
        for j, shift in enumerate(shifts):
            of = source_of(me_ref[0], shift, n)

            @pl.when((cols_ref[of] == b) & (live_ref[of] != 0))
            def _():
                weights = tiles_ref[of]
                for t in range(steps):
                    acc[t] += mm_tn(weights, parts[j][t])

        out_ref[...] = acc[...].astype(BF16)

    line = pl.BlockSpec((steps, tile, width), lambda b: (0, b, 0))
    piece = pl.BlockSpec((steps, tile, width), lambda b: (0, 0, 0))
    every = pl.BlockSpec(tiles.shape, lambda b: (0, 0, 0))
    size = steps * assets * width
    return pl.pallas_call(
        body,
        grid=(blocks,),
        out_shape=jax.ShapeDtypeStruct(base.shape, BF16),
        in_specs=[SMEM, SMEM, SMEM, every, line] + [piece] * count,
        out_specs=line,
        scratch_shapes=[pltpu.VMEM((steps, tile, width), F32)],
        compiler_params=params(32),
        cost_estimate=cost(2 * size * tile, 10 * size),
        name="finish",
    )(me, cols, live, tiles, base, *returned)


def levels(tm, asset):
    low = max(d for d in range(1, math.isqrt(asset) + 1) if asset % d == 0)
    pair = 2 if tm % 2 == 0 else 1
    return [("tm", 1, pair, tm), ("tm", pair, tm // pair, tm), ("asset", 1, low, asset), ("asset", low, asset // low, asset)]


def member(level):
    axis, stride, size, _ = level
    return (lax.axis_index(axis) // stride) % size


def pairs_of(level, shift):
    _, stride, size, n = level
    return [(i, i + ((i // stride + shift) % size - (i // stride) % size) * stride) for i in range(n)]


def scatter_sum(x, level):
    axis, _, size, _ = level
    me = member(level)
    total = lax.dynamic_index_in_dim(x, me, 0, keepdims=False)
    arrived = [
        lax.ppermute(lax.dynamic_index_in_dim(x, (me + s) % size, 0, keepdims=False), axis, pairs_of(level, s))
        for s in range(1, size)
    ]
    for part in arrived:
        total = total + part
    return total


def spread(x, level):
    axis, _, size, _ = level
    return jnp.stack([x] + [lax.ppermute(x, axis, pairs_of(level, s)) for s in range(1, size)])


def unshuffle(x, order, shape):
    sizes = [level[2] for level in order]
    place = jnp.arange(math.prod(sizes), dtype=jnp.int32)
    index, stride = 0, 1
    for level in reversed(order):
        size = level[2]
        index = index + ((member(level) - place // stride) % size) * stride
        stride *= size
    flat = x.reshape(math.prod(sizes), -1, shape[1])
    return jnp.take(flat, index, axis=0, mode="clip").reshape(shape).astype(F32)


def per_device(
    features,
    w_value,
    w_gate,
    cotangent,
    local_rows,
    local_cols,
    local_count,
    local_tiles,
    remote_rows,
    remote_cols,
    remote_live,
    remote_tiles,
):
    steps, assets, width = features.shape
    tile = local_tiles.shape[1]
    n = lax.axis_size("asset")
    tm = lax.axis_size("tm")
    me = lax.axis_index("asset").astype(jnp.int32).reshape(1)
    flat = features.reshape(-1, width)
    grad = cotangent.reshape(-1, width)

    far = list(range(n // 2, n))
    near = list(range(1, n // 2))
    shifts = far + near

    sent = dict(zip(shifts, send_forward(me, features, remote_tiles, remote_cols, remote_live, shifts, n)))
    came = {}
    for j, s in enumerate(far):
        came[s] = exchange(sent[s] if j < 2 else after(sent[s], came[far[j - 2]]), s, n)
    for j, s in enumerate(near):
        came[s] = exchange(sent[s] if j < 3 else after(sent[s], came[near[j - 3]]), s, n)

    gate, dagg, back = project(flat, grad, w_value, w_gate)
    back_steps = back.reshape(features.shape)
    owed = dict(zip(shifts, send_backward(me, back_steps, remote_rows, shifts, n, tile)))
    local = local_sum(local_tiles, local_count, local_rows, local_cols, features, None)
    base = local_sum(local_tiles, local_count, local_cols, local_rows, back_steps, cotangent)

    half = len(far) // 2
    got = {}
    for j, s in enumerate(far[:half]):
        got[s] = exchange(after(owed[s], came[far[half + j]]), s, n)

    total, part_value = gather_sum(
        me, local, [came[s] for s in shifts], remote_rows, dagg.reshape(features.shape), shifts, n, tile
    )
    output, dgate, part_gate = mix(total.reshape(-1, width), w_value, gate, flat, grad)
    base = add_gate(base.reshape(-1, width), dgate, w_gate).reshape(features.shape)

    order = levels(tm, n)
    sizes = [level[2] for level in order]
    rows = width // math.prod(sizes)
    sums = [part.reshape(sizes + [rows, width]) for part in (part_value, part_gate)]
    for level in order[:-1]:
        sums = [scatter_sum(x, level) for x in sums]
    both = jnp.concatenate(sums, axis=1)
    both = scatter_sum(both, order[-1]).astype(BF16)
    both = spread(both, order[-1])
    for j, s in enumerate(far[half:]):
        got[s] = exchange(after(owed[s], both), s, n)
    for j, s in enumerate(near):
        got[s] = exchange(after(owed[s], both), s, n)
    for level in reversed(order[:-1]):
        both = spread(both, level)
    both = both.reshape(math.prod(sizes), 2, rows, width)
    scale = float(steps * assets * tm * n) ** (-0.5)
    grad_value, grad_gate = [unshuffle(both[:, i], order, (width, width)) * scale for i in range(2)]

    grad_features = finish(
        me, base, [got[s] for s in shifts], remote_cols, remote_live, remote_tiles, shifts, n
    )
    return output.reshape(features.shape), grad_features, grad_value, grad_gate


def solution(mesh):
    return jax.shard_map(
        per_device,
        mesh=mesh,
        in_specs=(
            P("tm", "asset", None),
            P(),
            P(),
            P("tm", "asset", None),
            P("asset"),
            P("asset"),
            P("asset"),
            P("asset", None, None),
            P("asset"),
            P("asset"),
            P("asset"),
            P("asset", None, None),
        ),
        out_specs=(P("tm", "asset", None), P("tm", "asset", None), P(), P()),
        check_vma=False,
    )
```

```python
import math

import jax
import jax.numpy as jnp
from jax import lax
from jax.experimental import pallas as pl
from jax.experimental.pallas import tpu as pltpu
from jax.sharding import PartitionSpec as P

F32 = jnp.float32
BF16 = jnp.bfloat16
ANY = pl.BlockSpec(memory_space=pl.ANY)
VMEM = pl.BlockSpec(memory_space=pltpu.VMEM)
SMEM = pl.BlockSpec(memory_space=pltpu.SMEM)
MIB = 1 << 20


def params(mib=16):
    return pltpu.CompilerParams(vmem_limit_bytes=mib * MIB)


def cost(flops, moved):
    return pl.CostEstimate(flops=int(flops), bytes_accessed=int(moved), transcendentals=0)


def mm(a, b):
    return lax.dot_general(a, b, (((1,), (0,)), ((), ())), preferred_element_type=F32)


def mm_tn(a, b):
    return lax.dot_general(a, b, (((0,), (0,)), ((), ())), preferred_element_type=F32)


def mm_nt(a, b):
    return lax.dot_general(a, b, (((1,), (1,)), ((), ())), preferred_element_type=F32)


def far_memory(*arrays):
    return [x if x.dtype == jnp.int32 else pltpu.with_memory_space_constraint(x, pltpu.HBM) for x in arrays]


def flat_rows(x):
    return x.reshape(-1, x.shape[-1])


def after(x, *others):
    return lax.optimization_barrier((x,) + others)[0]


def row_chunk(rows, most):
    return max(c for c in range(8, most + 1, 8) if rows % c == 0)


def target_of(index, shift, n):
    return index ^ shift if n & (n - 1) == 0 else (index + shift) % n


def source_of(index, shift, n):
    return index ^ shift if n & (n - 1) == 0 else (index + n - shift) % n


def exchange(block, shift, n):
    return lax.ppermute(block, "asset", [(i, target_of(i, shift, n)) for i in range(n)])


def send_forward(me, features, tiles, cols, live, shifts, n):
    steps, _, width = features.shape
    tile = tiles.shape[1]
    count = len(shifts)

    def body(me_ref, cols_ref, live_ref, tiles_ref, f_ref, *rest):
        outs, (weights, blocks, made, tile_sem, block_sem, made_sem) = rest[:count], rest[count:]
        loads = []
        for j, shift in enumerate(shifts):
            to = target_of(me_ref[0], shift, n)
            start = pl.multiple_of(cols_ref[to] * tile, tile)
            load = (
                pltpu.make_async_copy(tiles_ref.at[to], weights.at[j], tile_sem.at[j]),
                pltpu.make_async_copy(f_ref.at[:, pl.ds(start, tile), :], blocks.at[j], block_sem.at[j]),
            )
            for copy in load:
                copy.start()
            loads.append(load)
        stores = []
        for j, shift in enumerate(shifts):
            to = target_of(me_ref[0], shift, n)
            for copy in loads[j]:
                copy.wait()
            used = weights[j] * live_ref[to].astype(F32).astype(BF16)
            for t in range(steps):
                made[j, t] = mm(used, blocks[j, t]).astype(BF16)
            store = pltpu.make_async_copy(made.at[j], outs[j], made_sem.at[j])
            store.start()
            stores.append(store)
        for store in stores:
            store.wait()

    block = pltpu.HBM((steps, tile, width), BF16)
    size = steps * tile * width
    many = pltpu.VMEM((count, steps, tile, width), BF16)
    sems = pltpu.SemaphoreType.DMA((count,))
    return pl.pallas_call(
        body,
        out_shape=[block] * count,
        in_specs=[SMEM, SMEM, SMEM, ANY, ANY],
        out_specs=[ANY] * count,
        scratch_shapes=[pltpu.VMEM((count, tile, tile), BF16), many, many, sems, sems, sems],
        compiler_params=params(),
        cost_estimate=cost(2 * count * size * tile, 4 * count * size),
        name="send_forward",
    )(*far_memory(me, cols, live, tiles, features))


def send_backward(back, rows, tile):
    steps, _, width = back.shape
    n = rows.shape[0]

    def body(rows_ref, r_ref, *rest):
        outs, (held, load_sem, store_sem) = rest[:steps], rest[steps:]
        loads = []
        for s in range(n):
            at = pl.ds(pl.multiple_of(rows_ref[s] * tile, tile), tile)
            load = pltpu.make_async_copy(r_ref.at[:, at, :], held.at[:, s], load_sem.at[s])
            load.start()
            loads.append(load)
        for load in loads:
            load.wait()
        stores = [pltpu.make_async_copy(held.at[t], outs[t], store_sem.at[t]) for t in range(steps)]
        for store in stores:
            store.start()
        for store in stores:
            store.wait()

    return pl.pallas_call(
        body,
        out_shape=[pltpu.HBM((n, tile, width), BF16)] * steps,
        in_specs=[SMEM, ANY],
        out_specs=[ANY] * steps,
        scratch_shapes=[
            pltpu.VMEM((steps, n, tile, width), BF16),
            pltpu.SemaphoreType.DMA((n,)),
            pltpu.SemaphoreType.DMA((steps,)),
        ],
        compiler_params=params(),
        cost_estimate=cost(0, 0),
        name="send_backward",
    )(*far_memory(rows, back))


def project(flat, grad, w_value, w_gate):
    rows, width = flat.shape
    chunk = row_chunk(rows, 512)

    def body(f_ref, c_ref, wv_ref, wg_ref, back_ref):
        gate = jax.nn.sigmoid(mm(f_ref[...], wg_ref[...]))
        dagg = (c_ref[...].astype(F32) * gate).astype(BF16)
        back_ref[...] = mm_nt(dagg, wv_ref[...]).astype(BF16)

    line = pl.BlockSpec((chunk, width), lambda i: (i, 0))
    whole = pl.BlockSpec((width, width), lambda i: (0, 0))
    return pl.pallas_call(
        body,
        grid=(rows // chunk,),
        out_shape=pltpu.HBM((rows, width), BF16),
        in_specs=[line, line, whole, whole],
        out_specs=line,
        compiler_params=params(),
        cost_estimate=cost(0, 0),
        name="project",
    )(*far_memory(flat, grad, w_value, w_gate))


def place_tiles(dense, tiles_ref, count, rows_ref, cols_ref, turned):
    tile = tiles_ref.shape[1]
    dense[...] = jnp.zeros(dense.shape, BF16)

    @pl.loop(0, count)
    def _(l):
        row, col = (cols_ref[l], rows_ref[l]) if turned else (rows_ref[l], cols_ref[l])
        to = (pl.ds(pl.multiple_of(row * tile, tile), tile), pl.ds(pl.multiple_of(col * tile, tile), tile))
        new = tiles_ref[l].astype(F32)
        dense[to] = (dense[to].astype(F32) + (new.T if turned else new)).astype(BF16)


def gate_terms(f, c, g, wv, wg):
    gate = jax.nn.sigmoid(mm(f, wg))
    kept = gate * mm(g, wv)
    c = c.astype(F32)
    return kept, (c * gate).astype(BF16), (c * kept * (1.0 - gate)).astype(BF16)


def local_terms(step, sums, count, rows, cols, tiles, features, grad, back, w_value, w_gate):
    _, assets, width = features.shape
    _, tile, _ = tiles.shape
    chunk = row_chunk(assets, 2 * tile)

    def body(count_ref, rows_ref, cols_ref, tiles_ref, f_ref, r_ref, c_ref, wv_ref, wg_ref, *rest):
        o_ref, base_ref, sums_ref, dense, turned = rest[-5:]
        i = pl.program_id(0)

        @pl.when(i == 0)
        def _():
            place_tiles(dense, tiles_ref, count_ref[0], rows_ref, cols_ref, False)
            place_tiles(turned, tiles_ref, count_ref[0], rows_ref, cols_ref, True)
            sums_ref[...] = jnp.zeros(sums_ref.shape, F32) if sums is None else rest[0][...]

        at = pl.ds(pl.multiple_of(i * chunk, chunk), chunk)
        g = mm(dense[at, :], f_ref[0]).astype(BF16)
        f = f_ref[0, at, :]
        kept, dagg, dgate = gate_terms(f, c_ref[0], g, wv_ref[...], wg_ref[...])
        o_ref[...] = f.astype(F32) + kept
        base_ref[...] = c_ref[0].astype(F32) + mm(turned[at, :], r_ref[0]) + mm_nt(dgate, wg_ref[...])
        sums_ref[0] += mm_tn(g, dagg)
        sums_ref[1] += mm_tn(f, dgate)

    line = pl.BlockSpec((chunk, width), lambda i: (i, 0))
    slab = pl.BlockSpec((1, assets, width), lambda i: (step, 0, 0))
    weight = pl.BlockSpec((width, width), lambda i: (0, 0))
    whole = pl.BlockSpec((2, width, width), lambda i: (0, 0, 0))
    old = [] if sums is None else [sums]
    return pl.pallas_call(
        body,
        grid=(assets // chunk,),
        out_shape=[pltpu.HBM((assets, width), F32)] * 2 + [pltpu.HBM((2, width, width), F32)],
        in_specs=[SMEM, SMEM, SMEM, pl.BlockSpec(tiles.shape, lambda i: (0, 0, 0)), slab, slab]
        + [pl.BlockSpec((1, chunk, width), lambda i: (step, i, 0)), weight, weight]
        + [whole] * len(old),
        out_specs=[line, line, whole],
        scratch_shapes=[pltpu.VMEM((assets, assets), BF16)] * 2,
        compiler_params=params(56),
        cost_estimate=cost(0, 0),
        name="local_terms",
    )(*far_memory(count, rows, cols, tiles, features, back, grad, w_value, w_gate, *old))


def add_arrived(me, sums, arrived, rows, features, grad, w_value, w_gate, shifts, n, tile):
    steps, _, width = features.shape
    count = len(shifts)

    def body(me_ref, rows_ref, s_ref, f_ref, c_ref, wv_ref, wg_ref, *rest):
        parts, (sums_ref, made_ref) = rest[:count], rest[count : count + 2]
        p_buf, f_buf, c_buf, w_buf, s_buf, made, sem, w_sem, made_sem = rest[count + 2 :]
        loads = [pltpu.make_async_copy(ref, w_buf.at[i], w_sem.at[i]) for i, ref in enumerate((wv_ref, wg_ref))]
        for j, shift in enumerate(shifts):
            row = rows_ref[source_of(me_ref[0], shift, n)]
            at = pl.ds(pl.multiple_of(row * tile, tile), tile)
            for i, (ref, buf) in enumerate(((f_ref.at[:, at, :], f_buf), (c_ref.at[:, at, :], c_buf), (parts[j], p_buf))):
                loads.append(pltpu.make_async_copy(ref, buf.at[j], sem.at[i, j]))
        old = pltpu.make_async_copy(s_ref, s_buf, w_sem.at[2])
        for load in loads:
            load.start()
        old.start()
        loads[0].wait()
        loads[1].wait()
        stores = []
        for j in range(count):
            for load in loads[2 + 3 * j : 5 + 3 * j]:
                load.wait()
            p, f, c = [flat_rows(buf[j]) for buf in (p_buf, f_buf, c_buf)]
            kept, dagg, dgate = gate_terms(f, c, p, w_buf[0], w_buf[1])
            made[j, 0] = kept.astype(BF16).reshape(steps, tile, width)
            made[j, 1] = dgate.reshape(steps, tile, width)
            store = pltpu.make_async_copy(made.at[j], made_ref.at[j], made_sem.at[j])
            store.start()
            stores.append(store)
            if j == 0:
                sums_ref[0] = mm_tn(p, dagg)
                sums_ref[1] = mm_tn(f, dgate)
            else:
                sums_ref[0] += mm_tn(p, dagg)
                sums_ref[1] += mm_tn(f, dgate)
        old.wait()
        sums_ref[...] += s_buf[...]
        for store in stores:
            store.wait()

    many = pltpu.VMEM((count, steps, tile, width), BF16)
    pair = (count, 2, steps, tile, width)
    return pl.pallas_call(
        body,
        out_shape=[pltpu.HBM(sums.shape, F32), pltpu.HBM(pair, BF16)],
        in_specs=[SMEM, SMEM] + [ANY] * (5 + count),
        out_specs=[VMEM, ANY],
        scratch_shapes=[
            many,
            many,
            many,
            pltpu.VMEM((2, width, width), BF16),
            pltpu.VMEM(sums.shape, F32),
            pltpu.VMEM(pair, BF16),
            pltpu.SemaphoreType.DMA((3, count)),
            pltpu.SemaphoreType.DMA((3,)),
            pltpu.SemaphoreType.DMA((count,)),
        ],
        compiler_params=params(48),
        cost_estimate=cost(0, 0),
        name="add_arrived",
    )(*far_memory(me, rows, sums, features, grad, w_value, w_gate, *arrived))


def settle(me, local, made, rows, groups, n, tile):
    steps = len(local)
    assets, width = local[0].shape
    blocks = assets // tile

    def body(me_ref, rows_ref, *rest):
        parts, (out_ref, acc) = rest[steps:-2], rest[-2:]
        b = pl.program_id(0)
        for t in range(steps):
            acc[t] = rest[t][...]
        for part, shifts in zip(parts, groups):
            for j, shift in enumerate(shifts):

                @pl.when(rows_ref[source_of(me_ref[0], shift, n)] == b)
                def _():
                    acc[...] += part[j, 0].astype(F32)

        out_ref[...] = acc[...].astype(BF16)

    line = pl.BlockSpec((tile, width), lambda b: (b, 0))
    pieces = [pl.BlockSpec((x.shape[0], 1) + x.shape[2:], lambda b: (0,) * 5) for x in made]
    return pl.pallas_call(
        body,
        grid=(blocks,),
        out_shape=pltpu.HBM((steps, assets, width), BF16),
        in_specs=[SMEM, SMEM] + [line] * steps + pieces,
        out_specs=pl.BlockSpec((steps, tile, width), lambda b: (0, b, 0)),
        scratch_shapes=[pltpu.VMEM((steps, tile, width), F32)],
        compiler_params=params(32),
        cost_estimate=cost(0, 0),
        name="settle",
    )(*far_memory(me, rows, *local, *made))


def finish(step, steps, grads, me, base, made, rows, groups, returned, cols, live, tiles, w_gate, n):
    assets, width = base.shape
    tile = tiles.shape[1]
    blocks = assets // tile
    sets = len(made)

    def body(me_ref, rows_ref, cols_ref, live_ref, tiles_ref, w_ref, r_ref, b_ref, *rest):
        dgates, (out_ref, acc) = rest[:sets], rest[-2:]
        b = pl.program_id(0)
        acc[...] = b_ref[...]
        for part, group in zip(dgates, groups):
            for j, shift in enumerate(group):

                @pl.when(rows_ref[source_of(me_ref[0], shift, n)] == b)
                def _():
                    acc[...] += mm_nt(part[j, 0, 0], w_ref[...])

        for of in range(n):

            @pl.when((cols_ref[of] == b) & (live_ref[of] != 0))
            def _():
                acc[...] += mm_tn(tiles_ref[of], r_ref[of])

        out_ref[0] = acc[...].astype(BF16)

    line = pl.BlockSpec((tile, width), lambda b: (b, 0))
    pieces = [pl.BlockSpec((x.shape[0], 1, 1) + x.shape[3:], lambda b: (0, 1, step, 0, 0)) for x in made]
    every = [pl.BlockSpec(x.shape, lambda b: (0, 0, 0)) for x in (tiles, returned)]
    weight = pl.BlockSpec((width, width), lambda b: (0, 0))
    old = [] if grads is None else [grads]
    return pl.pallas_call(
        body,
        grid=(blocks,),
        out_shape=pltpu.HBM((steps, assets, width), BF16),
        in_specs=[SMEM, SMEM, SMEM, SMEM, every[0], weight, every[1], line] + pieces + [ANY] * len(old),
        out_specs=pl.BlockSpec((1, tile, width), lambda b: (step, b, 0)),
        scratch_shapes=[pltpu.VMEM((tile, width), F32)],
        input_output_aliases={8 + sets: 0} if old else {},
        compiler_params=params(32),
        cost_estimate=cost(0, 0),
        name="finish",
    )(*far_memory(me, rows, cols, live, tiles, w_gate, returned, base, *made, *old))


def levels(tm, asset):
    low = max(d for d in range(1, math.isqrt(asset) + 1) if asset % d == 0)
    pair = 2 if tm % 2 == 0 else 1
    return [("tm", 1, pair, tm), ("tm", pair, tm // pair, tm), ("asset", 1, low, asset), ("asset", low, asset // low, asset)]


def member(level):
    axis, stride, size, _ = level
    return (lax.axis_index(axis) // stride) % size


def pairs_of(level, shift):
    _, stride, size, n = level
    return [(i, i + ((i // stride + shift) % size - (i // stride) % size) * stride) for i in range(n)]


def scatter_sum(x, level, wire):
    axis, _, size, _ = level
    me = member(level)
    total = lax.dynamic_index_in_dim(x, me, 0, keepdims=False)
    arrived = [
        lax.ppermute(lax.dynamic_index_in_dim(x, (me + s) % size, 0, keepdims=False).astype(wire), axis, pairs_of(level, s))
        for s in range(1, size)
    ]
    for part in arrived:
        total = total + part.astype(F32)
    return total


def spread(x, level):
    axis, _, size, _ = level
    return jnp.stack([x] + [lax.ppermute(x, axis, pairs_of(level, s)) for s in range(1, size)])


def unshuffle(x, order, shape):
    sizes = [level[2] for level in order]
    place = jnp.arange(math.prod(sizes), dtype=jnp.int32)
    index, stride = 0, 1
    for level in reversed(order):
        size = level[2]
        index = index + ((member(level) - place // stride) % size) * stride
        stride *= size
    flat = x.reshape(math.prod(sizes), -1, shape[-1])
    return jnp.take(flat, index, axis=0, mode="clip").reshape(shape).astype(F32)


def per_device(
    features,
    w_value,
    w_gate,
    cotangent,
    local_rows,
    local_cols,
    local_count,
    local_tiles,
    remote_rows,
    remote_cols,
    remote_live,
    remote_tiles,
):
    steps, assets, width = features.shape
    tile = local_tiles.shape[1]
    n = lax.axis_size("asset")
    tm = lax.axis_size("tm")
    me = lax.axis_index("asset").astype(jnp.int32).reshape(1)
    flat = features.reshape(-1, width)
    grad = cotangent.reshape(-1, width)

    far = list(range(n // 2, n))
    near = list(range(1, n // 2))
    shifts = far + near
    half = len(far) // 2
    first, second = far[:half] + near[:1], far[half:] + near[1:]
    late = far[half:]
    early = [s for s in shifts if s not in late]
    weights = (w_value, w_gate)
    graph = (local_count, local_rows, local_cols, local_tiles)

    sent = dict(zip(shifts, send_forward(me, features, remote_tiles, remote_cols, remote_live, shifts, n)))
    came = {s: exchange(sent[s], s, n) for s in first}
    back = project(flat, grad, *weights).reshape(features.shape)
    out, base = [None] * steps, [None] * steps
    out[0], base[0], sums = local_terms(0, None, *graph, features, cotangent, back, *weights)
    for s in second:
        came[s] = exchange(after(sent[s], sums, *[came[i] for i in first]), s, n)
    rest = [after(x, *[came[i] for i in first]) for x in (features, cotangent)]
    for t in range(1, steps):
        out[t], base[t], sums = local_terms(t, sums, *graph, *rest, back, *weights)
    owed = send_backward(back, remote_rows, tile)
    sums, made_early = add_arrived(
        me, sums, [came[s] for s in early], remote_rows, *rest, *weights, early, n, tile
    )
    sums, made_late = add_arrived(
        me, after(sums, *owed), [came[s] for s in late], remote_rows, *rest, *weights, late, n, tile
    )
    made, groups = (made_early, made_late), (early, late)

    order = levels(tm, n)
    sizes = [level[2] for level in order]
    rows = 2 * width // math.prod(sizes)

    def send_back(t, *before):
        return lax.all_to_all(after(owed[t], *before), "asset", 0, 0, tiled=True)

    returned = [send_back(t, *[came[s] for s in late]) for t in range(steps // 2)]
    output = settle(me, out, made, remote_rows, groups, n, tile)
    sums = scatter_sum(sums.reshape(sizes + [rows, width]), order[0], F32)
    sums = scatter_sum(sums, order[1], BF16)
    sums = after(scatter_sum(sums, order[2], BF16), output, *returned)
    sums = scatter_sum(sums, order[3], BF16).astype(BF16)
    sums = spread(sums, order[3])
    returned += [send_back(t, sums) for t in range(steps // 2, steps)]

    grad_features = None

    def finish_step(t):
        return finish(
            t, steps, grad_features, me, base[t], made, remote_rows, groups, returned[t], remote_cols, remote_live,
            remote_tiles, w_gate, n
        )

    for t in range(steps // 2):
        grad_features = finish_step(t)
    sums = spread(sums, order[2])
    sums = spread(sums, order[1])
    if grad_features is not None:
        sums = after(sums, grad_features)
    sums = spread(sums, order[0])
    scale = float(steps * assets * tm * n) ** (-0.5)
    sums = unshuffle(sums, order, (2, width, width)) * scale
    for t in range(steps // 2, steps):
        grad_features = finish_step(t)
    return output, grad_features, sums[0], sums[1]


def solution(mesh):
    return jax.shard_map(
        per_device,
        mesh=mesh,
        in_specs=(
            P("tm", "asset", None),
            P(),
            P(),
            P("tm", "asset", None),
            P("asset"),
            P("asset"),
            P("asset"),
            P("asset", None, None),
            P("asset"),
            P("asset"),
            P("asset"),
            P("asset", None, None),
        ),
        out_specs=(P("tm", "asset", None), P("tm", "asset", None), P(), P()),
        check_vma=False,
    )
```

```python
import math

import jax
import jax.numpy as jnp
from jax import lax
from jax.experimental import pallas as pl
from jax.experimental.pallas import tpu as pltpu
from jax.sharding import PartitionSpec as P

F32 = jnp.float32
BF16 = jnp.bfloat16
ANY = pl.BlockSpec(memory_space=pl.ANY)
VMEM = pl.BlockSpec(memory_space=pltpu.VMEM)
SMEM = pl.BlockSpec(memory_space=pltpu.SMEM)
MIB = 1 << 20


def params(mib=40):
    return pltpu.CompilerParams(vmem_limit_bytes=mib * MIB)


def cost(flops, moved):
    return pl.CostEstimate(flops=int(flops), bytes_accessed=int(moved), transcendentals=0)


def mm(a, b):
    return lax.dot_general(a, b, (((1,), (0,)), ((), ())), preferred_element_type=F32)


def mm_tn(a, b):
    return lax.dot_general(a, b, (((0,), (0,)), ((), ())), preferred_element_type=F32)


def mm_nt(a, b):
    return lax.dot_general(a, b, (((1,), (1,)), ((), ())), preferred_element_type=F32)


def far_memory(*arrays):
    return [pltpu.with_memory_space_constraint(x, pltpu.HBM) for x in arrays]


def id_memory(n, count):
    return [pltpu.SMEM((n,), jnp.int32)] * count + [pltpu.SemaphoreType.DMA((count,))]


def id_copies(sources, buffers, sem):
    copies = [pltpu.make_async_copy(source, buffer, sem.at[i]) for i, (source, buffer) in enumerate(zip(sources, buffers))]
    for copy in copies:
        copy.start()
    return copies


def flat_rows(x):
    return x.reshape(-1, x.shape[-1])


def after(x, *others):
    return lax.optimization_barrier((x,) + others)[0]


def row_chunk(rows, most):
    return max(c for c in range(8, most + 1, 8) if rows % c == 0)


def target_of(index, shift, n):
    return index ^ shift if n & (n - 1) == 0 else (index + shift) % n


def source_of(index, shift, n):
    return index ^ shift if n & (n - 1) == 0 else (index + n - shift) % n


def exchange(block, shift, n):
    return lax.ppermute(block, "asset", [(i, target_of(i, shift, n)) for i in range(n)])


def send_forward(me, features, tiles, cols, live, shifts, n):
    steps, _, width = features.shape
    tile = tiles.shape[1]
    count = len(shifts)

    def body(me_ref, cols_in, live_in, tiles_ref, f_ref, *rest):
        outs, (weights, blocks, made, tile_sem, block_sem, made_sem) = rest[:count], rest[count : count + 6]
        cols_ref, live_ref, id_sem = rest[count + 6 :]
        ids = id_copies((cols_in, live_in), (cols_ref, live_ref), id_sem)
        loads = []
        for j, shift in enumerate(shifts):
            to = target_of(me_ref[0], shift, n)
            loads.append([pltpu.make_async_copy(tiles_ref.at[to], weights.at[j], tile_sem.at[j])])
            loads[j][0].start()
        for copy in ids:
            copy.wait()
        for j, shift in enumerate(shifts):
            start = pl.multiple_of(cols_ref[target_of(me_ref[0], shift, n)] * tile, tile)
            loads[j].append(pltpu.make_async_copy(f_ref.at[:, pl.ds(start, tile), :], blocks.at[j], block_sem.at[j]))
            loads[j][1].start()
        stores = []
        for j, shift in enumerate(shifts):
            to = target_of(me_ref[0], shift, n)
            for copy in loads[j]:
                copy.wait()
            used = weights[j] * live_ref[to].astype(F32).astype(BF16)
            for t in range(steps):
                made[j, t] = mm(used, blocks[j, t]).astype(BF16)
            store = pltpu.make_async_copy(made.at[j], outs[j], made_sem.at[j])
            store.start()
            stores.append(store)
        for store in stores:
            store.wait()

    block = pltpu.HBM((steps, tile, width), BF16)
    size = steps * tile * width
    many = pltpu.VMEM((count, steps, tile, width), BF16)
    sems = pltpu.SemaphoreType.DMA((count,))
    return pl.pallas_call(
        body,
        out_shape=[block] * count,
        in_specs=[SMEM, ANY, ANY, ANY, ANY],
        out_specs=[ANY] * count,
        scratch_shapes=[pltpu.VMEM((count, tile, tile), BF16), many, many, sems, sems, sems] + id_memory(n, 2),
        compiler_params=params(),
        cost_estimate=cost(2 * count * size * tile, 4 * count * size),
        name="send_forward",
    )(me, *far_memory(cols, live, tiles, features))


def place_tiles(dense, tiles_ref, count, rows_ref, cols_ref, turned):
    tile = tiles_ref.shape[1]
    dense[...] = jnp.zeros(dense.shape, BF16)

    @pl.loop(0, count)
    def _(l):
        row, col = (cols_ref[l], rows_ref[l]) if turned else (rows_ref[l], cols_ref[l])
        to = (pl.ds(pl.multiple_of(row * tile, tile), tile), pl.ds(pl.multiple_of(col * tile, tile), tile))
        new = tiles_ref[l].astype(F32)
        dense[to] = (dense[to].astype(F32) + (new.T if turned else new)).astype(BF16)


def gate_terms(f, c, g, wv, wg):
    gate = jax.nn.sigmoid(mm(f, wg))
    kept = gate * mm(g, wv)
    c = c.astype(F32)
    return kept, (c * gate).astype(BF16), (c * kept * (1.0 - gate)).astype(BF16)


def load_ids(sources, buffers, sem):
    for copy in id_copies(sources, buffers, sem):
        copy.wait()


def local_forward(count, rows, cols, tiles, features, grad, w_value, w_gate, wanted):
    steps, assets, width = features.shape
    tile = tiles.shape[1]
    n = wanted.shape[0]
    chunk = row_chunk(assets, 5 * tile)
    turns = assets // chunk

    def body(count_ref, rows_ref, cols_ref, wanted_ref, tiles_ref, c_ref, wv_ref, wg_ref, f_in, *rest):
        kept_ref, dgate_ref, back_ref, sums_ref = rest[:4]
        owed, (dense, f_ref, r_ref, sem, r_sem) = rest[4 : 4 + steps], rest[4 + steps :]
        t, i = pl.program_id(0), pl.program_id(1)
        loads = [pltpu.make_async_copy(f_in.at[s], f_ref.at[s], sem.at[s]) for s in range(steps)]

        @pl.when((t == 0) & (i == 0))
        def _():
            for load in loads:
                load.start()
            place_tiles(dense, tiles_ref, count_ref[0], rows_ref, cols_ref, False)
            sums_ref[...] = jnp.zeros(sums_ref.shape, F32)

        for s in range(steps):

            @pl.when((t == s) & (i == 0))
            def _():
                loads[s].wait()

        at = pl.ds(pl.multiple_of(i * chunk, chunk), chunk)
        f = f_ref[t, at, :]
        g = mm(dense[at, :], f_ref[t]).astype(BF16)
        kept, dagg, dgate = gate_terms(f, c_ref[0], g, wv_ref[...], wg_ref[...])
        back = mm_nt(dagg, wv_ref[...]).astype(BF16)
        back_ref[0] = back
        r_ref[at, :] = back
        kept_ref[0] = kept.astype(BF16)
        dgate_ref[0] = dgate
        sums_ref[0] += mm_tn(g, dagg)
        sums_ref[1] += mm_tn(f, dgate)

        @pl.when(i == turns - 1)
        def _():
            for s in range(steps):

                @pl.when(t == s)
                def _():
                    stores = []
                    for d in range(n):
                        block = pl.ds(pl.multiple_of(wanted_ref[d] * tile, tile), tile)
                        stores.append(pltpu.make_async_copy(r_ref.at[block, :], owed[s].at[d], r_sem.at[d]))
                    for store in stores:
                        store.start()
                    for store in stores:
                        store.wait()

    line = pl.BlockSpec((1, chunk, width), lambda t, i: (t, i, 0))
    weight = pl.BlockSpec((width, width), lambda t, i: (0, 0))
    return pl.pallas_call(
        body,
        grid=(steps, turns),
        out_shape=[pltpu.HBM(features.shape, BF16)] * 3
        + [pltpu.HBM((2, width, width), F32)]
        + [pltpu.HBM((n, tile, width), BF16)] * steps,
        in_specs=[SMEM] * 4 + [pl.BlockSpec(tiles.shape, lambda t, i: (0, 0, 0)), line, weight, weight, ANY],
        out_specs=[line, line, line, pl.BlockSpec((2, width, width), lambda t, i: (0, 0, 0))] + [ANY] * steps,
        scratch_shapes=[
            pltpu.VMEM((assets, assets), BF16),
            pltpu.VMEM(features.shape, BF16),
            pltpu.VMEM((assets, width), BF16),
            pltpu.SemaphoreType.DMA((steps,)),
            pltpu.SemaphoreType.DMA((n,)),
        ],
        compiler_params=params(),
        cost_estimate=cost(0, 0),
        name="local_forward",
    )(count, rows, cols, wanted, *far_memory(tiles, grad, w_value, w_gate, features))


def local_back(me, count, rows, cols, tiles, back, grad, dgate, made, places, groups, w_gate, n):
    steps, assets, width = back.shape
    tile = tiles.shape[1]
    chunk = row_chunk(assets, 5 * tile)
    per = chunk // tile
    sets = len(made)

    def body(me_ref, count_ref, rows_ref, cols_ref, places_ref, tiles_ref, c_ref, d_ref, w_ref, r_in, *rest):
        parts, (out_ref, dense, r_ref, sem, *turned) = rest[:sets], rest[sets:]
        t, i = pl.program_id(0), pl.program_id(1)
        loads = [pltpu.make_async_copy(r_in.at[s], r_ref.at[s], sem.at[s]) for s in range(steps)]

        @pl.when((t == 0) & (i == 0))
        def _():
            for load in loads:
                load.start()
            place_tiles(dense, tiles_ref, count_ref[0], rows_ref, cols_ref, True)
            for part, to in zip(parts, turned):
                to[...] = mm_nt(flat_rows(part[...]), w_ref[...]).reshape(to.shape)

        for s in range(steps):

            @pl.when((t == s) & (i == 0))
            def _():
                loads[s].wait()

        at = pl.ds(pl.multiple_of(i * chunk, chunk), chunk)
        out_ref[0] = c_ref[0].astype(F32) + mm(dense[at, :], r_ref[t]) + mm_nt(d_ref[0], w_ref[...])
        for part, shifts in zip(turned, groups):
            for j, shift in enumerate(shifts):
                place = places_ref[source_of(me_ref[0], shift, n)] - i * per

                @pl.when((place >= 0) & (place < per))
                def _():
                    out_ref[0, pl.ds(pl.multiple_of(place * tile, tile), tile), :] += part[j, t]

    line = pl.BlockSpec((1, chunk, width), lambda t, i: (t, i, 0))
    weight = pl.BlockSpec((width, width), lambda t, i: (0, 0))
    pieces = [pl.BlockSpec((x.shape[0], 1) + x.shape[2:], lambda t, i: (0, 1, 0, 0, 0)) for x in made]
    return pl.pallas_call(
        body,
        grid=(steps, assets // chunk),
        out_shape=pltpu.HBM(back.shape, F32),
        in_specs=[SMEM] * 5
        + [pl.BlockSpec(tiles.shape, lambda t, i: (0, 0, 0)), line, line, weight, ANY]
        + pieces,
        out_specs=line,
        scratch_shapes=[
            pltpu.VMEM((assets, assets), BF16),
            pltpu.VMEM(back.shape, BF16),
            pltpu.SemaphoreType.DMA((steps,)),
        ]
        + [pltpu.VMEM((x.shape[0],) + x.shape[2:], F32) for x in made],
        compiler_params=params(),
        cost_estimate=cost(0, 0),
        name="local_back",
    )(me, count, rows, cols, places, *far_memory(tiles, grad, dgate, w_gate, back, *made))


def add_arrived(me, sums, arrived, rows, features, grad, w_value, w_gate, shifts, n, tile):
    steps, _, width = features.shape
    count = len(shifts)
    most = 3
    summed = sums is not None

    def body(me_ref, rows_in, f_ref, c_ref, wv_ref, wg_ref, *rest):
        parts, rest = rest[:count], rest[count:]
        if summed:
            s_ref, made_ref, sums_ref, s_buf, *rest = rest
        else:
            made_ref, *rest = rest
        p_buf, f_buf, c_buf, w_buf, made, sem, w_sem, made_sem, rows_ref, id_sem = rest
        ids = id_copies((rows_in,), (rows_ref,), id_sem)
        first = [pltpu.make_async_copy(ref, w_buf.at[i], w_sem.at[i]) for i, ref in enumerate((wg_ref, wv_ref))]
        first += [pltpu.make_async_copy(parts[j], p_buf.at[j], sem.at[0, j]) for j in range(count)]
        for load in first:
            load.start()
        ids[0].wait()
        then = []
        for j, shift in enumerate(shifts):
            at = pl.ds(pl.multiple_of(rows_ref[source_of(me_ref[0], shift, n)] * tile, tile), tile)
            then.append(pltpu.make_async_copy(f_ref.at[:, at, :], f_buf.at[j], sem.at[1, j]))
            then.append(pltpu.make_async_copy(c_ref.at[:, at, :], c_buf.at[j], sem.at[2, j]))
        for load in then:
            load.start()
        if summed:
            old = pltpu.make_async_copy(s_ref, s_buf, w_sem.at[2])
            old.start()
        for load in first:
            load.wait()
        stores = []
        for low in range(0, count, most):
            some = slice(low, min(low + most, count))
            for load in then[2 * some.start : 2 * some.stop]:
                load.wait()
            p, f, c = [flat_rows(buf[some]) for buf in (p_buf, f_buf, c_buf)]
            kept, dagg, dgate = gate_terms(f, c, p, w_buf[1], w_buf[0])
            shape = (some.stop - some.start, steps, tile, width)
            made[some, 0] = kept.astype(BF16).reshape(shape)
            made[some, 1] = dgate.reshape(shape)
            store = pltpu.make_async_copy(made.at[some], made_ref.at[some], made_sem.at[low])
            store.start()
            stores.append(store)
            if summed and low == 0:
                old.wait()
                sums_ref[0] = s_buf[0] + mm_tn(p, dagg)
                sums_ref[1] = s_buf[1] + mm_tn(f, dgate)
            elif summed:
                sums_ref[0] += mm_tn(p, dagg)
                sums_ref[1] += mm_tn(f, dgate)
        for store in stores:
            store.wait()

    many = pltpu.VMEM((count, steps, tile, width), BF16)
    pair = (count, 2, steps, tile, width)
    operands = far_memory(rows, features, grad, w_value, w_gate) + list(arrived)
    out_shape, out_specs, scratch = [pltpu.HBM(pair, BF16)], [ANY], []
    if summed:
        operands += far_memory(sums)
        out_shape.append(pltpu.HBM(sums.shape, F32))
        out_specs.append(VMEM)
        scratch.append(pltpu.VMEM(sums.shape, F32))
    return pl.pallas_call(
        body,
        out_shape=out_shape,
        in_specs=[SMEM] + [ANY] * len(operands),
        out_specs=out_specs,
        scratch_shapes=scratch
        + [
            many,
            many,
            many,
            pltpu.VMEM((2, width, width), BF16),
            pltpu.VMEM(pair, BF16),
            pltpu.SemaphoreType.DMA((3, count)),
            pltpu.SemaphoreType.DMA((3,)),
            pltpu.SemaphoreType.DMA((count,)),
        ]
        + id_memory(n, 1),
        compiler_params=params(),
        cost_estimate=cost(0, 0),
        name="add_arrived" if summed else "arrived_terms",
    )(me, *operands)


def prepare_late(me, rows, features, grad, w_gate, shifts, n, tile):
    steps, _, width = features.shape
    count = len(shifts)

    def body(me_ref, rows_in, f_ref, c_ref, w_ref, half_ref, u_ref, f_buf, c_buf, sem, rows_ref, id_sem):
        load_ids((rows_in,), (rows_ref,), id_sem)
        loads = []
        for j, shift in enumerate(shifts):
            at = pl.ds(pl.multiple_of(rows_ref[source_of(me_ref[0], shift, n)] * tile, tile), tile)
            loads.append(pltpu.make_async_copy(f_ref.at[:, at, :], f_buf.at[j], sem.at[0, j]))
            loads.append(pltpu.make_async_copy(c_ref.at[:, at, :], c_buf.at[j], sem.at[1, j]))
        for load in loads:
            load.start()
        for load in loads:
            load.wait()
        f = flat_rows(f_buf[...])
        gate = jax.nn.sigmoid(mm(f, w_ref[...]))
        dagg = flat_rows(c_buf[...]).astype(F32) * gate
        half_ref[0] = f
        half_ref[1] = dagg.astype(BF16)
        u_ref[...] = dagg * (1.0 - gate)

    many = pltpu.VMEM((count, steps, tile, width), BF16)
    lines = count * steps * tile
    return pl.pallas_call(
        body,
        out_shape=[pltpu.HBM((2, lines, width), BF16), pltpu.HBM((lines, width), F32)],
        in_specs=[SMEM, ANY, ANY, ANY, VMEM],
        out_specs=[VMEM, VMEM],
        scratch_shapes=[many, many, pltpu.SemaphoreType.DMA((2, count))] + id_memory(n, 1),
        compiler_params=params(),
        cost_estimate=cost(0, 0),
        name="prepare_late",
    )(me, *far_memory(rows, features, grad, w_gate))


def add_late(sums, arrived, half, u, w_value, place, level, wire):
    steps, tile, width = arrived[0].shape
    count = len(arrived)
    size = level[2]
    lines = 2 * width // size

    def body(place_ref, s_ref, half_ref, u_ref, w_ref, *rest):
        parts, (keep_ref, *send_refs), rest = rest[:count], rest[count : count + size], rest[count + size :]
        p_buf, w_buf, h_buf, u_buf, total, made, sem, done_sem = rest
        first = [pltpu.make_async_copy(parts[j], p_buf.at[j], sem.at[4 + j]) for j in range(count)]
        first += [pltpu.make_async_copy(ref, buf, sem.at[i]) for i, (ref, buf) in enumerate(((w_ref, w_buf), (half_ref, h_buf)))]
        later = [pltpu.make_async_copy(ref, buf, sem.at[2 + i]) for i, (ref, buf) in enumerate(((u_ref, u_buf), (s_ref, total)))]
        for load in first + later:
            load.start()
        for load in first:
            load.wait()
        p = flat_rows(p_buf[...])
        agg = mm(p, w_buf[...])
        value = mm_tn(p, h_buf[1])
        later[0].wait()
        gate = mm_tn(h_buf[0], (agg * u_buf[...]).astype(BF16))
        later[1].wait()
        total[:width, :] += value
        total[width:, :] += gate
        made[...] = total[...].astype(wire)
        stores = []
        for i, (source, to) in enumerate([(total, keep_ref)] + [(made, ref) for ref in send_refs]):
            mine = pl.ds(pl.multiple_of(lax.rem(place_ref[0] + i, size) * lines, lines), lines)
            stores.append(pltpu.make_async_copy(source.at[mine, :], to, done_sem.at[i]))
        for store in stores:
            store.start()
        for store in stores:
            store.wait()

    return pl.pallas_call(
        body,
        out_shape=[pltpu.HBM((lines, width), F32)] + [pltpu.HBM((lines, width), wire)] * (size - 1),
        in_specs=[SMEM] + [ANY] * (4 + count),
        out_specs=[ANY] * size,
        scratch_shapes=[
            pltpu.VMEM((count, steps, tile, width), BF16),
            pltpu.VMEM((width, width), BF16),
            pltpu.VMEM(half.shape, BF16),
            pltpu.VMEM(u.shape, F32),
            pltpu.VMEM((2 * width, width), F32),
            pltpu.VMEM((2 * width, width), wire),
            pltpu.SemaphoreType.DMA((4 + count,)),
            pltpu.SemaphoreType.DMA((size,)),
        ],
        compiler_params=params(),
        cost_estimate=cost(0, 0),
        name="add_late",
    )(place, *far_memory(sums.reshape(2 * width, width), half, u, w_value), *arrived)


def settle(me, kept, features, made, rows, groups, n, tile):
    steps, assets, width = kept.shape
    blocks = assets // tile
    per = 2 if blocks % 2 == 0 else 1
    sets = len(made)

    def body(me_ref, rows_ref, k_ref, f_ref, *rest):
        parts, (out_ref, acc) = rest[:sets], rest[sets:]
        b = pl.program_id(0)
        acc[...] = f_ref[...].astype(F32) + k_ref[...].astype(F32)
        for part, shifts in zip(parts, groups):
            for j, shift in enumerate(shifts):
                place = rows_ref[source_of(me_ref[0], shift, n)] - b * per

                @pl.when((place >= 0) & (place < per))
                def _():
                    acc[:, pl.ds(pl.multiple_of(place * tile, tile), tile), :] += part[j, 0].astype(F32)

        out_ref[...] = acc[...].astype(BF16)

    line = pl.BlockSpec((steps, per * tile, width), lambda b: (0, b, 0))
    pieces = [pl.BlockSpec((x.shape[0], 1) + x.shape[2:], lambda b: (0,) * 5) for x in made]
    return pl.pallas_call(
        body,
        grid=(blocks // per,),
        out_shape=pltpu.HBM((steps, assets, width), BF16),
        in_specs=[SMEM, SMEM, line, line] + pieces,
        out_specs=line,
        scratch_shapes=[pltpu.VMEM((steps, per * tile, width), F32)],
        compiler_params=params(),
        cost_estimate=cost(0, 0),
        name="settle",
    )(me, rows, *far_memory(kept, features, *made))


def finish(step, grads, base, returned, cols, live, tiles, n):
    steps, assets, width = base.shape
    tile = tiles.shape[1]
    blocks = assets // tile
    per = 2 if blocks % 2 == 0 else 1

    def body(cols_ref, live_ref, tiles_ref, r_ref, b_ref, *rest):
        out_ref, acc = rest[-2:]
        b = pl.program_id(0)
        acc[...] = b_ref[0]
        for of in range(n):
            spot = cols_ref[of] - b * per

            @pl.when((spot >= 0) & (spot < per) & (live_ref[of] != 0))
            def _():
                acc[pl.ds(pl.multiple_of(spot * tile, tile), tile), :] += mm_tn(tiles_ref[of], r_ref[of])

        out_ref[0] = acc[...].astype(BF16)

    line = pl.BlockSpec((1, per * tile, width), lambda b: (step, b, 0))
    every = [pl.BlockSpec(x.shape, lambda b: (0, 0, 0)) for x in (tiles, returned)]
    old = [] if grads is None else far_memory(grads)
    return pl.pallas_call(
        body,
        grid=(blocks // per,),
        out_shape=pltpu.HBM((steps, assets, width), BF16),
        in_specs=[SMEM, SMEM, *every, line] + [ANY] * len(old),
        out_specs=line,
        scratch_shapes=[pltpu.VMEM((per * tile, width), F32)],
        input_output_aliases={5: 0} if old else {},
        compiler_params=params(),
        cost_estimate=cost(0, 0),
        name="finish",
    )(cols, live, *far_memory(tiles), returned, *far_memory(base), *old)


def levels(tm, asset):
    low = max(d for d in range(1, math.isqrt(asset) + 1) if asset % d == 0)
    pair = 2 if tm % 2 == 0 else 1
    return [("tm", 1, pair, tm), ("tm", pair, tm // pair, tm), ("asset", 1, low, asset), ("asset", low, asset // low, asset)]


def member(level):
    axis, stride, size, _ = level
    return (lax.axis_index(axis) // stride) % size


def pairs_of(level, shift):
    _, stride, size, n = level
    return [(i, i + ((i // stride + shift) % size - (i // stride) % size) * stride) for i in range(n)]


def scatter_sum(terms, level, wire):
    axis, _, size, _ = level
    me = member(level)

    def entry(index):
        return sum(lax.dynamic_index_in_dim(x, index, 0, keepdims=False) for x in terms)

    arrived = [lax.ppermute(entry((me + s) % size).astype(wire), axis, pairs_of(level, s)) for s in range(1, size)]
    total = entry(me)
    for part in arrived:
        total = total + part.astype(F32)
    return total


def butterfly_sum(x, level, wire):
    axis, _, size, _ = level
    if size & (size - 1):
        return lax.psum(x, axis, axis_index_groups=groups_of(level))
    shift = 1
    while shift < size:
        x = x.astype(wire)
        x = x.astype(F32) + lax.ppermute(x, axis, [(i, i ^ (shift * level[1])) for i in range(level[3])]).astype(F32)
        shift *= 2
    return x


def groups_of(level):
    _, stride, size, n = level
    return [[i + s * stride for s in range(size)] for i in range(n) if (i // stride) % size == 0]


def spread(x, level):
    axis, _, size, _ = level
    return [x] + [lax.ppermute(x, axis, pairs_of(level, s)) for s in range(1, size)]


def unshuffle(x, stacked, placed, shape):
    place = jnp.arange(math.prod(level[2] for level in placed), dtype=jnp.int32)
    digits, stride = {}, 1
    for level in reversed(placed):
        digits[level] = (place // stride) % level[2]
        stride *= level[2]
    index, stride = 0, 1
    for level in reversed(stacked):
        index = index + ((member(level) - digits[level]) % level[2]) * stride
        stride *= level[2]
    flat = x.reshape(place.shape[0], -1, shape[-1])
    return jnp.take(flat, index, axis=0, mode="clip").reshape(shape).astype(F32)


def per_device(
    features,
    w_value,
    w_gate,
    cotangent,
    local_rows,
    local_cols,
    local_count,
    local_tiles,
    remote_rows,
    remote_cols,
    remote_live,
    remote_tiles,
):
    steps, assets, width = features.shape
    tile = local_tiles.shape[1]
    n = lax.axis_size("asset")
    tm = lax.axis_size("tm")
    me = lax.axis_index("asset").astype(jnp.int32).reshape(1)
    flat = features.reshape(-1, width)
    grad = cotangent.reshape(-1, width)

    far = list(range(n // 2, n))
    near = list(range(1, n // 2))
    shifts = far + near
    lead = max(1, len(far) - 1)
    first, second = far[:lead] + near[:2], far[lead:] + near[2:]
    late = far[-2:] + near[2:]
    early = [s for s in shifts if s not in late]
    weights = (w_value, w_gate)
    graph = (local_count, local_rows, local_cols, local_tiles)

    sent = dict(zip(shifts, send_forward(me, features, remote_tiles, remote_cols, remote_live, shifts, n)))
    came = {s: exchange(sent[s], s, n) for s in first}
    kept, dgate, back, sums, *owed = local_forward(*graph, features, cotangent, *weights, remote_rows)
    for s in second:
        came[s] = exchange(after(sent[s], sums, came[far[0]], came[near[0]]), s, n)
    half_late, u_late = prepare_late(me, remote_rows, features, cotangent, w_gate, late, n, tile)
    made_early, sums = add_arrived(
        me, sums, [came[s] for s in early], remote_rows, features, cotangent, *weights, early, n, tile
    )
    pair, column, row, line = levels(tm, n)
    whole = ("tm", 1, tm, tm)
    place = member(whole).astype(jnp.int32).reshape(1)
    keep, *sends = add_late(sums, [came[s] for s in late], half_late, u_late, w_value, place, whole, BF16)

    def send_back(t, *before):
        return lax.all_to_all(after(owed[t], *before), "asset", 0, 0, tiled=True)

    returned = [send_back(t, made_early, half_late, *[came[s] for s in late]) for t in range(steps // 2)]
    (made_late,) = add_arrived(
        me, None, [came[s] for s in late], remote_rows, features, cotangent, *weights, late, n, tile
    )
    made, groups = (made_early, made_late), (early, late)
    output = settle(me, kept, features, made, remote_rows, groups, n, tile)
    base = local_back(me, *graph, back, cotangent, dgate, made, remote_rows, groups, w_gate, n)
    terms = [keep] + [lax.ppermute(x, "tm", pairs_of(whole, i + 1)) for i, x in enumerate(sends)]
    terms[1] = after(terms[1], made_late, output)
    shape = (row[2], keep.shape[0] // row[2], width)
    terms = [x.astype(F32).reshape(shape) for x in terms]
    sums = after(scatter_sum(terms, row, BF16), *returned)
    sums = butterfly_sum(sums, line, BF16).astype(BF16)
    returned += [send_back(t, sums) for t in range(steps // 2, steps)]

    grad_features = None

    def finish_step(t):
        return finish(t, grad_features, base, returned[t], remote_cols, remote_live, remote_tiles, n)

    for t in range(steps // 2):
        grad_features = finish_step(t)
    sums = jnp.stack(spread(sums, row))
    sums = jnp.stack(spread(sums, column))
    if grad_features is not None:
        sums = after(sums, grad_features)
    sums = jnp.stack(spread(sums, pair))
    scale = float(steps * assets * tm * n) ** (-0.5)
    sums = unshuffle(sums, [pair, column, row], [column, pair, row], (2, width, width)) * scale
    for t in range(steps // 2, steps):
        grad_features = finish_step(t)
    return output, grad_features, sums[0], sums[1]


def solution(mesh):
    return jax.shard_map(
        per_device,
        mesh=mesh,
        in_specs=(
            P("tm", "asset", None),
            P(),
            P(),
            P("tm", "asset", None),
            P("asset"),
            P("asset"),
            P("asset"),
            P("asset", None, None),
            P("asset"),
            P("asset"),
            P("asset"),
            P("asset", None, None),
        ),
        out_specs=(P("tm", "asset", None), P("tm", "asset", None), P(), P()),
        check_vma=False,
    )
```

```python
import math

import jax
import jax.numpy as jnp
from jax import lax
from jax.experimental import pallas as pl
from jax.experimental.pallas import tpu as pltpu
from jax.sharding import PartitionSpec as P

F32 = jnp.float32
BF16 = jnp.bfloat16
ANY = pl.BlockSpec(memory_space=pl.ANY)
VMEM = pl.BlockSpec(memory_space=pltpu.VMEM)
SMEM = pl.BlockSpec(memory_space=pltpu.SMEM)
MIB = 1 << 20


def params(mib=40):
    return pltpu.CompilerParams(vmem_limit_bytes=mib * MIB)


def cost(flops, moved):
    return pl.CostEstimate(flops=int(flops), bytes_accessed=int(moved), transcendentals=0)


def mm(a, b):
    return lax.dot_general(a, b, (((1,), (0,)), ((), ())), preferred_element_type=F32)


def mm_tn(a, b):
    return lax.dot_general(a, b, (((0,), (0,)), ((), ())), preferred_element_type=F32)


def mm_nt(a, b):
    return lax.dot_general(a, b, (((1,), (1,)), ((), ())), preferred_element_type=F32)


def far_memory(*arrays):
    return [pltpu.with_memory_space_constraint(x, pltpu.HBM) for x in arrays]


def id_memory(n, count):
    return [pltpu.SMEM((n,), jnp.int32)] * count + [pltpu.SemaphoreType.DMA((count,))]


def id_copies(sources, buffers, sem):
    copies = [pltpu.make_async_copy(source, buffer, sem.at[i]) for i, (source, buffer) in enumerate(zip(sources, buffers))]
    for copy in copies:
        copy.start()
    return copies


def flat_rows(x):
    return x.reshape(-1, x.shape[-1])


def after(x, *others):
    return lax.optimization_barrier((x,) + others)[0]


def row_chunk(rows, most):
    return max(c for c in range(8, most + 1, 8) if rows % c == 0)


def target_of(index, shift, n):
    return index ^ shift if n & (n - 1) == 0 else (index + shift) % n


def source_of(index, shift, n):
    return index ^ shift if n & (n - 1) == 0 else (index + n - shift) % n


def exchange(block, shift, n):
    return lax.ppermute(block, "asset", [(i, target_of(i, shift, n)) for i in range(n)])


def send_forward(me, features, tiles, cols, live, shifts, n):
    steps, _, width = features.shape
    tile = tiles.shape[1]
    count = len(shifts)

    def body(me_ref, cols_in, live_in, tiles_ref, f_ref, *rest):
        outs, (weights, blocks, made, tile_sem, block_sem, made_sem) = rest[:count], rest[count : count + 6]
        cols_ref, live_ref, id_sem = rest[count + 6 :]
        ids = id_copies((cols_in, live_in), (cols_ref, live_ref), id_sem)
        loads = []
        for j, shift in enumerate(shifts):
            to = target_of(me_ref[0], shift, n)
            loads.append([pltpu.make_async_copy(tiles_ref.at[to], weights.at[j], tile_sem.at[j])])
            loads[j][0].start()
        for copy in ids:
            copy.wait()
        for j, shift in enumerate(shifts):
            start = pl.multiple_of(cols_ref[target_of(me_ref[0], shift, n)] * tile, tile)
            loads[j].append(pltpu.make_async_copy(f_ref.at[:, pl.ds(start, tile), :], blocks.at[j], block_sem.at[j]))
            loads[j][1].start()
        stores = []
        for j, shift in enumerate(shifts):
            to = target_of(me_ref[0], shift, n)
            for copy in loads[j]:
                copy.wait()
            used = weights[j] * live_ref[to].astype(F32).astype(BF16)
            for t in range(steps):
                made[j, t] = mm(used, blocks[j, t]).astype(BF16)
            store = pltpu.make_async_copy(made.at[j], outs[j], made_sem.at[j])
            store.start()
            stores.append(store)
        for store in stores:
            store.wait()

    block = pltpu.HBM((steps, tile, width), BF16)
    size = steps * tile * width
    many = pltpu.VMEM((count, steps, tile, width), BF16)
    sems = pltpu.SemaphoreType.DMA((count,))
    return pl.pallas_call(
        body,
        out_shape=[block] * count,
        in_specs=[SMEM, ANY, ANY, ANY, ANY],
        out_specs=[ANY] * count,
        scratch_shapes=[pltpu.VMEM((count, tile, tile), BF16), many, many, sems, sems, sems] + id_memory(n, 2),
        compiler_params=params(),
        cost_estimate=cost(2 * count * size * tile, 4 * count * size),
        name="send_forward",
    )(me, *far_memory(cols, live, tiles, features))


def place_tiles(dense, tiles_ref, count, rows_ref, cols_ref, turned):
    tile = tiles_ref.shape[1]
    dense[...] = jnp.zeros(dense.shape, BF16)

    @pl.loop(0, count)
    def _(l):
        row, col = (cols_ref[l], rows_ref[l]) if turned else (rows_ref[l], cols_ref[l])
        to = (pl.ds(pl.multiple_of(row * tile, tile), tile), pl.ds(pl.multiple_of(col * tile, tile), tile))
        new = tiles_ref[l].astype(F32)
        dense[to] = (dense[to].astype(F32) + (new.T if turned else new)).astype(BF16)


def gate_terms(f, c, g, wv, wg):
    gate = jax.nn.sigmoid(mm(f, wg))
    kept = gate * mm(g, wv)
    c = c.astype(F32)
    return kept, (c * gate).astype(BF16), (c * kept * (1.0 - gate)).astype(BF16)


def load_ids(sources, buffers, sem):
    for copy in id_copies(sources, buffers, sem):
        copy.wait()


def local_forward(count, rows, cols, tiles, features, grad, w_value, w_gate, wanted):
    steps, assets, width = features.shape
    tile = tiles.shape[1]
    n = wanted.shape[0]
    chunk = row_chunk(assets, 5 * tile)
    turns = assets // chunk

    def body(count_ref, rows_ref, cols_ref, wanted_ref, tiles_ref, c_ref, wv_ref, wg_ref, f_in, *rest):
        kept_ref, dgate_ref, back_ref, sums_ref = rest[:4]
        owed, (dense, f_ref, r_ref, sem, r_sem) = rest[4 : 4 + steps], rest[4 + steps :]
        t, i = pl.program_id(0), pl.program_id(1)
        loads = [pltpu.make_async_copy(f_in.at[s], f_ref.at[s], sem.at[s]) for s in range(steps)]

        @pl.when((t == 0) & (i == 0))
        def _():
            for load in loads:
                load.start()
            place_tiles(dense, tiles_ref, count_ref[0], rows_ref, cols_ref, False)
            sums_ref[...] = jnp.zeros(sums_ref.shape, F32)

        for s in range(steps):

            @pl.when((t == s) & (i == 0))
            def _():
                loads[s].wait()

        at = pl.ds(pl.multiple_of(i * chunk, chunk), chunk)
        f = f_ref[t, at, :]
        g = mm(dense[at, :], f_ref[t]).astype(BF16)
        kept, dagg, dgate = gate_terms(f, c_ref[0], g, wv_ref[...], wg_ref[...])
        back = mm_nt(dagg, wv_ref[...]).astype(BF16)
        back_ref[0] = back
        r_ref[at, :] = back
        kept_ref[0] = kept.astype(BF16)
        dgate_ref[0] = dgate
        sums_ref[0] += mm_tn(g, dagg)
        sums_ref[1] += mm_tn(f, dgate)

        @pl.when(i == turns - 1)
        def _():
            for s in range(steps):

                @pl.when(t == s)
                def _():
                    stores = []
                    for d in range(n):
                        block = pl.ds(pl.multiple_of(wanted_ref[d] * tile, tile), tile)
                        stores.append(pltpu.make_async_copy(r_ref.at[block, :], owed[s].at[d], r_sem.at[d]))
                    for store in stores:
                        store.start()
                    for store in stores:
                        store.wait()

    line = pl.BlockSpec((1, chunk, width), lambda t, i: (t, i, 0))
    weight = pl.BlockSpec((width, width), lambda t, i: (0, 0))
    return pl.pallas_call(
        body,
        grid=(steps, turns),
        out_shape=[pltpu.HBM(features.shape, BF16)] * 3
        + [pltpu.HBM((2, width, width), F32)]
        + [pltpu.HBM((n, tile, width), BF16)] * steps,
        in_specs=[SMEM] * 4 + [pl.BlockSpec(tiles.shape, lambda t, i: (0, 0, 0)), line, weight, weight, ANY],
        out_specs=[line, line, line, pl.BlockSpec((2, width, width), lambda t, i: (0, 0, 0))] + [ANY] * steps,
        scratch_shapes=[
            pltpu.VMEM((assets, assets), BF16),
            pltpu.VMEM(features.shape, BF16),
            pltpu.VMEM((assets, width), BF16),
            pltpu.SemaphoreType.DMA((steps,)),
            pltpu.SemaphoreType.DMA((n,)),
        ],
        compiler_params=params(),
        cost_estimate=cost(0, 0),
        name="local_forward",
    )(count, rows, cols, wanted, *far_memory(tiles, grad, w_value, w_gate, features))


def local_back(me, count, rows, cols, tiles, back, grad, dgate, made, places, groups, w_gate, n):
    steps, assets, width = back.shape
    tile = tiles.shape[1]
    chunk = row_chunk(assets, 5 * tile)
    per = chunk // tile
    sets = len(made)

    def body(me_ref, count_ref, rows_ref, cols_ref, places_ref, tiles_ref, c_ref, d_ref, w_ref, r_in, *rest):
        parts, (out_ref, dense, r_ref, sem, *turned) = rest[:sets], rest[sets:]
        t, i = pl.program_id(0), pl.program_id(1)
        loads = [pltpu.make_async_copy(r_in.at[s], r_ref.at[s], sem.at[s]) for s in range(steps)]

        @pl.when((t == 0) & (i == 0))
        def _():
            for load in loads:
                load.start()
            place_tiles(dense, tiles_ref, count_ref[0], rows_ref, cols_ref, True)
            for part, to in zip(parts, turned):
                to[...] = mm_nt(flat_rows(part[...]), w_ref[...]).reshape(to.shape)

        for s in range(steps):

            @pl.when((t == s) & (i == 0))
            def _():
                loads[s].wait()

        at = pl.ds(pl.multiple_of(i * chunk, chunk), chunk)
        out_ref[0] = c_ref[0].astype(F32) + mm(dense[at, :], r_ref[t]) + mm_nt(d_ref[0], w_ref[...])
        for part, shifts in zip(turned, groups):
            for j, shift in enumerate(shifts):
                place = places_ref[source_of(me_ref[0], shift, n)] - i * per

                @pl.when((place >= 0) & (place < per))
                def _():
                    out_ref[0, pl.ds(pl.multiple_of(place * tile, tile), tile), :] += part[j, t]

    line = pl.BlockSpec((1, chunk, width), lambda t, i: (t, i, 0))
    weight = pl.BlockSpec((width, width), lambda t, i: (0, 0))
    pieces = [pl.BlockSpec((x.shape[0], 1) + x.shape[2:], lambda t, i: (0, 1, 0, 0, 0)) for x in made]
    return pl.pallas_call(
        body,
        grid=(steps, assets // chunk),
        out_shape=pltpu.HBM(back.shape, F32),
        in_specs=[SMEM] * 5
        + [pl.BlockSpec(tiles.shape, lambda t, i: (0, 0, 0)), line, line, weight, ANY]
        + pieces,
        out_specs=line,
        scratch_shapes=[
            pltpu.VMEM((assets, assets), BF16),
            pltpu.VMEM(back.shape, BF16),
            pltpu.SemaphoreType.DMA((steps,)),
        ]
        + [pltpu.VMEM((x.shape[0],) + x.shape[2:], F32) for x in made],
        compiler_params=params(),
        cost_estimate=cost(0, 0),
        name="local_back",
    )(me, count, rows, cols, places, *far_memory(tiles, grad, dgate, w_gate, back, *made))


def add_arrived(me, sums, arrived, rows, features, grad, w_value, w_gate, shifts, n, tile):
    steps, _, width = features.shape
    count = len(shifts)
    most = 3
    summed = True

    def body(me_ref, rows_in, f_ref, c_ref, wv_ref, wg_ref, *rest):
        parts, rest = rest[:count], rest[count:]
        if summed:
            s_ref, made_ref, sums_ref, s_buf, *rest = rest
        else:
            made_ref, *rest = rest
        p_buf, f_buf, c_buf, w_buf, made, sem, w_sem, made_sem, rows_ref, id_sem = rest
        ids = id_copies((rows_in,), (rows_ref,), id_sem)
        first = [pltpu.make_async_copy(ref, w_buf.at[i], w_sem.at[i]) for i, ref in enumerate((wg_ref, wv_ref))]
        first += [pltpu.make_async_copy(parts[j], p_buf.at[j], sem.at[0, j]) for j in range(count)]
        for load in first:
            load.start()
        ids[0].wait()
        then = []
        for j, shift in enumerate(shifts):
            at = pl.ds(pl.multiple_of(rows_ref[source_of(me_ref[0], shift, n)] * tile, tile), tile)
            then.append(pltpu.make_async_copy(f_ref.at[:, at, :], f_buf.at[j], sem.at[1, j]))
            then.append(pltpu.make_async_copy(c_ref.at[:, at, :], c_buf.at[j], sem.at[2, j]))
        for load in then:
            load.start()
        if summed:
            old = pltpu.make_async_copy(s_ref, s_buf, w_sem.at[2])
            old.start()
        for load in first:
            load.wait()
        stores = []
        for low in range(0, count, most):
            some = slice(low, min(low + most, count))
            for load in then[2 * some.start : 2 * some.stop]:
                load.wait()
            p, f, c = [flat_rows(buf[some]) for buf in (p_buf, f_buf, c_buf)]
            kept, dagg, dgate = gate_terms(f, c, p, w_buf[1], w_buf[0])
            shape = (some.stop - some.start, steps, tile, width)
            made[some, 0] = kept.astype(BF16).reshape(shape)
            made[some, 1] = dgate.reshape(shape)
            store = pltpu.make_async_copy(made.at[some], made_ref.at[some], made_sem.at[low])
            store.start()
            stores.append(store)
            if summed and low == 0:
                old.wait()
                sums_ref[0] = s_buf[0] + mm_tn(p, dagg)
                sums_ref[1] = s_buf[1] + mm_tn(f, dgate)
            elif summed:
                sums_ref[0] += mm_tn(p, dagg)
                sums_ref[1] += mm_tn(f, dgate)
        for store in stores:
            store.wait()

    many = pltpu.VMEM((count, steps, tile, width), BF16)
    pair = (count, 2, steps, tile, width)
    operands = far_memory(rows, features, grad, w_value, w_gate) + list(arrived)
    out_shape, out_specs, scratch = [pltpu.HBM(pair, BF16)], [ANY], []
    if summed:
        operands += far_memory(sums)
        out_shape.append(pltpu.HBM(sums.shape, F32))
        out_specs.append(VMEM)
        scratch.append(pltpu.VMEM(sums.shape, F32))
    return pl.pallas_call(
        body,
        out_shape=out_shape,
        in_specs=[SMEM] + [ANY] * len(operands),
        out_specs=out_specs,
        scratch_shapes=scratch
        + [
            many,
            many,
            many,
            pltpu.VMEM((2, width, width), BF16),
            pltpu.VMEM(pair, BF16),
            pltpu.SemaphoreType.DMA((3, count)),
            pltpu.SemaphoreType.DMA((3,)),
            pltpu.SemaphoreType.DMA((count,)),
        ]
        + id_memory(n, 1),
        compiler_params=params(),
        cost_estimate=cost(0, 0),
        name="add_arrived" if summed else "arrived_terms",
    )(me, *operands)


def add_late(me, sums, arrived, rows, features, grad, w_value, w_gate, shifts, n, tile, place, level, wire):
    steps, _, width = features.shape
    count = len(shifts)
    size = level[2]
    lines = 2 * width // size

    def body(me_ref, place_ref, rows_in, f_ref, c_ref, wv_ref, wg_ref, s_ref, *rest):
        parts, (keep_ref, *send_refs), made_ref, rest = rest[:count], rest[count : count + size], rest[count + size], rest[count + size + 1 :]
        p_buf, f_buf, c_buf, w_buf, total, wired, made, sem, w_sem, done_sem, rows_ref, id_sem = rest
        ids = id_copies((rows_in,), (rows_ref,), id_sem)
        first = [pltpu.make_async_copy(ref, w_buf.at[i], w_sem.at[i]) for i, ref in enumerate((wg_ref, wv_ref))]
        first += [pltpu.make_async_copy(parts[j], p_buf.at[j], sem.at[0, j]) for j in range(count)]
        old = pltpu.make_async_copy(s_ref, total, w_sem.at[2])
        for load in first:
            load.start()
        ids[0].wait()
        then = []
        for j, shift in enumerate(shifts):
            at = pl.ds(pl.multiple_of(rows_ref[source_of(me_ref[0], shift, n)] * tile, tile), tile)
            then.append(pltpu.make_async_copy(f_ref.at[:, at, :], f_buf.at[j], sem.at[1, j]))
            then.append(pltpu.make_async_copy(c_ref.at[:, at, :], c_buf.at[j], sem.at[2, j]))
        for load in then:
            load.start()
        old.start()
        for load in first + then:
            load.wait()
        p, f, c = [flat_rows(buf[...]) for buf in (p_buf, f_buf, c_buf)]
        kept, dagg, dgate = gate_terms(f, c, p, w_buf[1], w_buf[0])
        value = mm_tn(p, dagg)
        gate = mm_tn(f, dgate)
        old.wait()
        total[:width, :] += value
        total[width:, :] += gate
        wired[...] = total[...].astype(wire)
        stores = []
        for i, (source, to) in enumerate([(total, keep_ref)] + [(wired, ref) for ref in send_refs]):
            mine = pl.ds(pl.multiple_of(lax.rem(place_ref[0] + i, size) * lines, lines), lines)
            stores.append(pltpu.make_async_copy(source.at[mine, :], to, done_sem.at[i]))
            stores[-1].start()
        shape = (count, steps, tile, width)
        made[:, 0] = kept.astype(BF16).reshape(shape)
        made[:, 1] = dgate.reshape(shape)
        stores.append(pltpu.make_async_copy(made, made_ref, done_sem.at[size]))
        stores[-1].start()
        for store in stores:
            store.wait()

    many = pltpu.VMEM((count, steps, tile, width), BF16)
    pair = (count, 2, steps, tile, width)
    return pl.pallas_call(
        body,
        out_shape=[pltpu.HBM((lines, width), F32)]
        + [pltpu.HBM((lines, width), wire)] * (size - 1)
        + [pltpu.HBM(pair, BF16)],
        in_specs=[SMEM, SMEM] + [ANY] * (6 + count),
        out_specs=[ANY] * (size + 1),
        scratch_shapes=[
            many,
            many,
            many,
            pltpu.VMEM((2, width, width), BF16),
            pltpu.VMEM((2 * width, width), F32),
            pltpu.VMEM((2 * width, width), wire),
            pltpu.VMEM(pair, BF16),
            pltpu.SemaphoreType.DMA((3, count)),
            pltpu.SemaphoreType.DMA((3,)),
            pltpu.SemaphoreType.DMA((size + 1,)),
        ]
        + id_memory(n, 1),
        compiler_params=params(),
        cost_estimate=cost(0, 0),
        name="add_late",
    )(me, place, *far_memory(rows, features, grad, w_value, w_gate, sums.reshape(2 * width, width)), *arrived)


def settle(me, kept, features, made, rows, groups, n, tile):
    steps, assets, width = kept.shape
    blocks = assets // tile
    per = 2 if blocks % 2 == 0 else 1
    sets = len(made)

    def body(me_ref, rows_ref, k_ref, f_ref, *rest):
        parts, (out_ref, acc) = rest[:sets], rest[sets:]
        b = pl.program_id(0)
        acc[...] = f_ref[...].astype(F32) + k_ref[...].astype(F32)
        for part, shifts in zip(parts, groups):
            for j, shift in enumerate(shifts):
                place = rows_ref[source_of(me_ref[0], shift, n)] - b * per

                @pl.when((place >= 0) & (place < per))
                def _():
                    acc[:, pl.ds(pl.multiple_of(place * tile, tile), tile), :] += part[j, 0].astype(F32)

        out_ref[...] = acc[...].astype(BF16)

    line = pl.BlockSpec((steps, per * tile, width), lambda b: (0, b, 0))
    pieces = [pl.BlockSpec((x.shape[0], 1) + x.shape[2:], lambda b: (0,) * 5) for x in made]
    return pl.pallas_call(
        body,
        grid=(blocks // per,),
        out_shape=pltpu.HBM((steps, assets, width), BF16),
        in_specs=[SMEM, SMEM, line, line] + pieces,
        out_specs=line,
        scratch_shapes=[pltpu.VMEM((steps, per * tile, width), F32)],
        compiler_params=params(),
        cost_estimate=cost(0, 0),
        name="settle",
    )(me, rows, *far_memory(kept, features, *made))


def finish(step, grads, base, returned, cols, live, tiles, n):
    steps, assets, width = base.shape
    tile = tiles.shape[1]
    blocks = assets // tile
    per = 2 if blocks % 2 == 0 else 1

    def body(cols_ref, live_ref, tiles_ref, r_ref, b_ref, *rest):
        out_ref, acc = rest[-2:]
        b = pl.program_id(0)
        acc[...] = b_ref[0]
        for of in range(n):
            spot = cols_ref[of] - b * per

            @pl.when((spot >= 0) & (spot < per) & (live_ref[of] != 0))
            def _():
                acc[pl.ds(pl.multiple_of(spot * tile, tile), tile), :] += mm_tn(tiles_ref[of], r_ref[of])

        out_ref[0] = acc[...].astype(BF16)

    line = pl.BlockSpec((1, per * tile, width), lambda b: (step, b, 0))
    every = [pl.BlockSpec(x.shape, lambda b: (0, 0, 0)) for x in (tiles, returned)]
    old = [] if grads is None else far_memory(grads)
    return pl.pallas_call(
        body,
        grid=(blocks // per,),
        out_shape=pltpu.HBM((steps, assets, width), BF16),
        in_specs=[SMEM, SMEM, *every, line] + [ANY] * len(old),
        out_specs=line,
        scratch_shapes=[pltpu.VMEM((per * tile, width), F32)],
        input_output_aliases={5: 0} if old else {},
        compiler_params=params(),
        cost_estimate=cost(0, 0),
        name="finish",
    )(cols, live, *far_memory(tiles), returned, *far_memory(base), *old)


def levels(tm, asset):
    low = max(d for d in range(1, math.isqrt(asset) + 1) if asset % d == 0)
    pair = 2 if tm % 2 == 0 else 1
    return [("tm", 1, pair, tm), ("tm", pair, tm // pair, tm), ("asset", 1, low, asset), ("asset", low, asset // low, asset)]


def member(level):
    axis, stride, size, _ = level
    return (lax.axis_index(axis) // stride) % size


def pairs_of(level, shift):
    _, stride, size, n = level
    return [(i, i + ((i // stride + shift) % size - (i // stride) % size) * stride) for i in range(n)]


def scatter_sum(terms, level, wire):
    axis, _, size, _ = level
    me = member(level)

    def entry(index):
        return sum(lax.dynamic_index_in_dim(x, index, 0, keepdims=False) for x in terms)

    arrived = [lax.ppermute(entry((me + s) % size).astype(wire), axis, pairs_of(level, s)) for s in range(1, size)]
    total = entry(me)
    for part in arrived:
        total = total + part.astype(F32)
    return total


def butterfly_sum(x, level, wire):
    axis, _, size, _ = level
    if size & (size - 1):
        return lax.psum(x, axis, axis_index_groups=groups_of(level))
    shift = 1
    while shift < size:
        x = x.astype(wire)
        x = x.astype(F32) + lax.ppermute(x, axis, [(i, i ^ (shift * level[1])) for i in range(level[3])]).astype(F32)
        shift *= 2
    return x


def groups_of(level):
    _, stride, size, n = level
    return [[i + s * stride for s in range(size)] for i in range(n) if (i // stride) % size == 0]


def spread(x, level):
    axis, _, size, _ = level
    return [x] + [lax.ppermute(x, axis, pairs_of(level, s)) for s in range(1, size)]


def unshuffle(x, stacked, placed, shape):
    place = jnp.arange(math.prod(level[2] for level in placed), dtype=jnp.int32)
    digits, stride = {}, 1
    for level in reversed(placed):
        digits[level] = (place // stride) % level[2]
        stride *= level[2]
    index, stride = 0, 1
    for level in reversed(stacked):
        index = index + ((member(level) - digits[level]) % level[2]) * stride
        stride *= level[2]
    flat = x.reshape(place.shape[0], -1, shape[-1])
    return jnp.take(flat, index, axis=0, mode="clip").reshape(shape).astype(F32)


def per_device(
    features,
    w_value,
    w_gate,
    cotangent,
    local_rows,
    local_cols,
    local_count,
    local_tiles,
    remote_rows,
    remote_cols,
    remote_live,
    remote_tiles,
):
    steps, assets, width = features.shape
    tile = local_tiles.shape[1]
    n = lax.axis_size("asset")
    tm = lax.axis_size("tm")
    me = lax.axis_index("asset").astype(jnp.int32).reshape(1)
    flat = features.reshape(-1, width)
    grad = cotangent.reshape(-1, width)

    far = list(range(n // 2, n))[::-1]
    near = list(range(1, n // 2))
    shifts = far + near
    lead = max(1, len(far) - 1)
    first, second = far[:lead] + near[:2], far[lead:] + near[2:]
    late = far[-2:] + near[2:]
    early = [s for s in shifts if s not in late]
    weights = (w_value, w_gate)
    graph = (local_count, local_rows, local_cols, local_tiles)

    sent = dict(zip(shifts, send_forward(me, features, remote_tiles, remote_cols, remote_live, shifts, n)))
    came = {s: exchange(sent[s], s, n) for s in first}
    kept, dgate, back, sums, *owed = local_forward(*graph, features, cotangent, *weights, remote_rows)
    for s in second:
        came[s] = exchange(after(sent[s], sums, came[far[0]], came[near[0]]), s, n)
    made_early, sums = add_arrived(
        me, sums, [came[s] for s in early], remote_rows, features, cotangent, *weights, early, n, tile
    )
    pair, column, row, line = levels(tm, n)
    whole = ("tm", 1, tm, tm)
    place = member(whole).astype(jnp.int32).reshape(1)
    keep, *sends, made_late = add_late(
        me, sums, [came[s] for s in late], remote_rows, features, cotangent, *weights, late, n, tile, place, whole, BF16
    )

    def send_back(t, *before):
        return lax.all_to_all(after(owed[t], *before), "asset", 0, 0, tiled=True)

    returned = [send_back(t, made_early, *[came[s] for s in late]) for t in range(steps // 2)]
    made, groups = (made_early, made_late), (early, late)
    output = settle(me, kept, features, made, remote_rows, groups, n, tile)
    base = local_back(me, *graph, back, cotangent, dgate, made, remote_rows, groups, w_gate, n)
    terms = [keep] + [lax.ppermute(x, "tm", pairs_of(whole, i + 1)) for i, x in enumerate(sends)]
    terms[1] = after(terms[1], base)
    shape = (row[2], keep.shape[0] // row[2], width)
    terms = [x.astype(F32).reshape(shape) for x in terms]
    sums = after(scatter_sum(terms, row, BF16), *returned)
    sums = butterfly_sum(sums, line, BF16).astype(BF16)
    returned += [send_back(t, sums) for t in range(steps // 2, steps)]

    grad_features = None

    def finish_step(t):
        return finish(t, grad_features, base, returned[t], remote_cols, remote_live, remote_tiles, n)

    for t in range(steps // 2):
        grad_features = finish_step(t)
    sums = jnp.stack(spread(sums, row))
    sums = jnp.stack(spread(sums, column))
    if grad_features is not None:
        sums = after(sums, grad_features, output)
    sums = jnp.stack(spread(sums, pair))
    scale = float(steps * assets * tm * n) ** (-0.5)
    sums = unshuffle(sums, [pair, column, row], [column, pair, row], (2, width, width)) * scale
    for t in range(steps // 2, steps):
        grad_features = finish_step(t)
    return output, grad_features, sums[0], sums[1]


def solution(mesh):
    return jax.shard_map(
        per_device,
        mesh=mesh,
        in_specs=(
            P("tm", "asset", None),
            P(),
            P(),
            P("tm", "asset", None),
            P("asset"),
            P("asset"),
            P("asset"),
            P("asset", None, None),
            P("asset"),
            P("asset"),
            P("asset"),
            P("asset", None, None),
        ),
        out_specs=(P("tm", "asset", None), P("tm", "asset", None), P(), P()),
        check_vma=False,
    )
```

```python
import math

import jax
import jax.numpy as jnp
from jax import lax
from jax.experimental import pallas as pl
from jax.experimental.pallas import tpu as pltpu
from jax.sharding import PartitionSpec as P

F32 = jnp.float32
BF16 = jnp.bfloat16
ANY = pl.BlockSpec(memory_space=pl.ANY)
VMEM = pl.BlockSpec(memory_space=pltpu.VMEM)
SMEM = pl.BlockSpec(memory_space=pltpu.SMEM)
MIB = 1 << 20


def params(mib=40):
    return pltpu.CompilerParams(vmem_limit_bytes=mib * MIB)


def cost(flops, moved):
    return pl.CostEstimate(flops=int(flops), bytes_accessed=int(moved), transcendentals=0)


def mm(a, b):
    return lax.dot_general(a, b, (((1,), (0,)), ((), ())), preferred_element_type=F32)


def mm_tn(a, b):
    return lax.dot_general(a, b, (((0,), (0,)), ((), ())), preferred_element_type=F32)


def mm_nt(a, b):
    return lax.dot_general(a, b, (((1,), (1,)), ((), ())), preferred_element_type=F32)


def far_memory(*arrays):
    return [pltpu.with_memory_space_constraint(x, pltpu.HBM) for x in arrays]


def id_memory(n, count):
    return [pltpu.SMEM((n,), jnp.int32)] * count + [pltpu.SemaphoreType.DMA((count,))]


def id_copies(sources, buffers, sem):
    copies = [pltpu.make_async_copy(source, buffer, sem.at[i]) for i, (source, buffer) in enumerate(zip(sources, buffers))]
    for copy in copies:
        copy.start()
    return copies


def flat_rows(x):
    return x.reshape(-1, x.shape[-1])


def after(x, *others):
    return lax.optimization_barrier((x,) + others)[0]


def row_chunk(rows, most):
    return max(c for c in range(8, most + 1, 8) if rows % c == 0)


def target_of(index, shift, n):
    return index ^ shift if n & (n - 1) == 0 else (index + shift) % n


def source_of(index, shift, n):
    return index ^ shift if n & (n - 1) == 0 else (index + n - shift) % n


def exchange(block, shift, n):
    return lax.ppermute(block, "asset", [(i, target_of(i, shift, n)) for i in range(n)])


def send_forward(me, features, tiles, cols, live, shifts, n):
    steps, _, width = features.shape
    tile = tiles.shape[1]
    count = len(shifts)

    def body(me_ref, cols_in, live_in, tiles_ref, f_ref, *rest):
        outs, (weights, blocks, made, tile_sem, block_sem, made_sem) = rest[:count], rest[count : count + 6]
        cols_ref, live_ref, id_sem = rest[count + 6 :]
        ids = id_copies((cols_in, live_in), (cols_ref, live_ref), id_sem)
        loads = []
        for j, shift in enumerate(shifts):
            to = target_of(me_ref[0], shift, n)
            loads.append([pltpu.make_async_copy(tiles_ref.at[to], weights.at[j], tile_sem.at[j])])
            loads[j][0].start()
        for copy in ids:
            copy.wait()
        for j, shift in enumerate(shifts):
            start = pl.multiple_of(cols_ref[target_of(me_ref[0], shift, n)] * tile, tile)
            loads[j].append(pltpu.make_async_copy(f_ref.at[:, pl.ds(start, tile), :], blocks.at[j], block_sem.at[j]))
            loads[j][1].start()
        stores = []
        for j, shift in enumerate(shifts):
            to = target_of(me_ref[0], shift, n)
            for copy in loads[j]:
                copy.wait()
            used = weights[j] * live_ref[to].astype(F32).astype(BF16)
            for t in range(steps):
                made[j, t] = mm(used, blocks[j, t]).astype(BF16)
            store = pltpu.make_async_copy(made.at[j], outs[j], made_sem.at[j])
            store.start()
            stores.append(store)
        for store in stores:
            store.wait()

    block = pltpu.HBM((steps, tile, width), BF16)
    size = steps * tile * width
    many = pltpu.VMEM((count, steps, tile, width), BF16)
    sems = pltpu.SemaphoreType.DMA((count,))
    return pl.pallas_call(
        body,
        out_shape=[block] * count,
        in_specs=[SMEM, ANY, ANY, ANY, ANY],
        out_specs=[ANY] * count,
        scratch_shapes=[pltpu.VMEM((count, tile, tile), BF16), many, many, sems, sems, sems] + id_memory(n, 2),
        compiler_params=params(),
        cost_estimate=cost(2 * count * size * tile, 4 * count * size),
        name="send_forward",
    )(me, *far_memory(cols, live, tiles, features))


def place_tiles(dense, tiles_ref, count, rows_ref, cols_ref, turned):
    tile = tiles_ref.shape[1]
    dense[...] = jnp.zeros(dense.shape, BF16)

    @pl.loop(0, count)
    def _(l):
        row, col = (cols_ref[l], rows_ref[l]) if turned else (rows_ref[l], cols_ref[l])
        to = (pl.ds(pl.multiple_of(row * tile, tile), tile), pl.ds(pl.multiple_of(col * tile, tile), tile))
        new = tiles_ref[l].astype(F32)
        dense[to] = (dense[to].astype(F32) + (new.T if turned else new)).astype(BF16)


def gate_terms(f, c, g, wv, wg):
    gate = jax.nn.sigmoid(mm(f, wg))
    kept = gate * mm(g, wv)
    c = c.astype(F32)
    return kept, (c * gate).astype(BF16), (c * kept * (1.0 - gate)).astype(BF16)


def load_ids(sources, buffers, sem):
    for copy in id_copies(sources, buffers, sem):
        copy.wait()


def local_forward(count, rows, cols, tiles, features, grad, w_value, w_gate, wanted):
    steps, assets, width = features.shape
    tile = tiles.shape[1]
    n = wanted.shape[0]
    chunk = row_chunk(assets, 5 * tile)
    turns = assets // chunk

    def body(count_ref, rows_ref, cols_ref, wanted_ref, tiles_ref, c_ref, wv_ref, wg_ref, f_in, *rest):
        kept_ref, dgate_ref, back_ref, sums_ref = rest[:4]
        owed, (dense, f_ref, r_ref, sem, r_sem) = rest[4 : 4 + steps], rest[4 + steps :]
        t, i = pl.program_id(0), pl.program_id(1)
        loads = [pltpu.make_async_copy(f_in.at[s], f_ref.at[s], sem.at[s]) for s in range(steps)]

        @pl.when((t == 0) & (i == 0))
        def _():
            for load in loads:
                load.start()
            place_tiles(dense, tiles_ref, count_ref[0], rows_ref, cols_ref, False)
            sums_ref[...] = jnp.zeros(sums_ref.shape, F32)

        for s in range(steps):

            @pl.when((t == s) & (i == 0))
            def _():
                loads[s].wait()

        at = pl.ds(pl.multiple_of(i * chunk, chunk), chunk)
        f = f_ref[t, at, :]
        g = mm(dense[at, :], f_ref[t]).astype(BF16)
        kept, dagg, dgate = gate_terms(f, c_ref[0], g, wv_ref[...], wg_ref[...])
        back = mm_nt(dagg, wv_ref[...]).astype(BF16)
        back_ref[0] = back
        r_ref[at, :] = back
        kept_ref[0] = kept.astype(BF16)
        dgate_ref[0] = dgate
        sums_ref[0] += mm_tn(g, dagg)
        sums_ref[1] += mm_tn(f, dgate)

        @pl.when(i == turns - 1)
        def _():
            for s in range(steps):

                @pl.when(t == s)
                def _():
                    stores = []
                    for d in range(n):
                        block = pl.ds(pl.multiple_of(wanted_ref[d] * tile, tile), tile)
                        stores.append(pltpu.make_async_copy(r_ref.at[block, :], owed[s].at[d], r_sem.at[d]))
                    for store in stores:
                        store.start()
                    for store in stores:
                        store.wait()

    line = pl.BlockSpec((1, chunk, width), lambda t, i: (t, i, 0))
    weight = pl.BlockSpec((width, width), lambda t, i: (0, 0))
    return pl.pallas_call(
        body,
        grid=(steps, turns),
        out_shape=[pltpu.HBM(features.shape, BF16)] * 3
        + [pltpu.HBM((2, width, width), F32)]
        + [pltpu.HBM((n, tile, width), BF16)] * steps,
        in_specs=[SMEM] * 4 + [pl.BlockSpec(tiles.shape, lambda t, i: (0, 0, 0)), line, weight, weight, ANY],
        out_specs=[line, line, line, pl.BlockSpec((2, width, width), lambda t, i: (0, 0, 0))] + [ANY] * steps,
        scratch_shapes=[
            pltpu.VMEM((assets, assets), BF16),
            pltpu.VMEM(features.shape, BF16),
            pltpu.VMEM((assets, width), BF16),
            pltpu.SemaphoreType.DMA((steps,)),
            pltpu.SemaphoreType.DMA((n,)),
        ],
        compiler_params=params(),
        cost_estimate=cost(0, 0),
        name="local_forward",
    )(count, rows, cols, wanted, *far_memory(tiles, grad, w_value, w_gate, features))


def local_back(me, count, rows, cols, tiles, back, grad, dgate, made, places, groups, w_gate, n):
    steps, assets, width = back.shape
    tile = tiles.shape[1]
    chunk = row_chunk(assets, 5 * tile)
    per = chunk // tile
    shapes = [(x.shape[0],) + x.shape[2:] for x in made]

    def body(me_ref, count_ref, rows_ref, cols_ref, places_ref, c_ref, d_ref, tiles_in, w_in, r_in, early_in, late_in, *rest):
        out_ref, dense, tiles_ref, w_ref, r_ref, early_ref, late_ref, turned, sem, r_sem = rest
        t, i = pl.program_id(0), pl.program_id(1)
        loads = [pltpu.make_async_copy(r_in.at[s], r_ref.at[s], r_sem.at[s]) for s in range(steps)]
        sides = ((tiles_in, tiles_ref), (w_in, w_ref), (late_in.at[:, 1], late_ref), (early_in.at[:, 1], early_ref))
        others = [pltpu.make_async_copy(source, to, sem.at[k]) for k, (source, to) in enumerate(sides)]

        @pl.when((t == 0) & (i == 0))
        def _():
            for load in others[:1] + loads[:1] + others[1:] + loads[1:]:
                load.start()
            others[0].wait()
            place_tiles(dense, tiles_ref, count_ref[0], rows_ref, cols_ref, True)
            for load in others[1:]:
                load.wait()
            turned[...] = mm_nt(flat_rows(late_ref[...]), w_ref[...]).reshape(turned.shape)

        for s in range(steps):

            @pl.when((t == s) & (i == 0))
            def _():
                loads[s].wait()

        at = pl.ds(pl.multiple_of(i * chunk, chunk), chunk)
        out_ref[0] = c_ref[0].astype(F32) + mm(dense[at, :], r_ref[t]) + mm_nt(d_ref[0], w_ref[...])
        for part, shifts in zip((early_ref, turned), groups):
            for j, shift in enumerate(shifts):
                place = places_ref[source_of(me_ref[0], shift, n)] - i * per

                @pl.when((place >= 0) & (place < per))
                def _():
                    out_ref[0, pl.ds(pl.multiple_of(place * tile, tile), tile), :] += part[j, t].astype(F32)

    line = pl.BlockSpec((1, chunk, width), lambda t, i: (t, i, 0))
    return pl.pallas_call(
        body,
        grid=(steps, assets // chunk),
        out_shape=pltpu.HBM(back.shape, F32),
        in_specs=[SMEM] * 5 + [line, line] + [ANY] * 5,
        out_specs=line,
        scratch_shapes=[
            pltpu.VMEM((assets, assets), BF16),
            pltpu.VMEM(tiles.shape, BF16),
            pltpu.VMEM(w_gate.shape, BF16),
            pltpu.VMEM(back.shape, BF16),
            pltpu.VMEM(shapes[0], BF16),
            pltpu.VMEM(shapes[1], BF16),
            pltpu.VMEM(shapes[1], F32),
            pltpu.SemaphoreType.DMA((4,)),
            pltpu.SemaphoreType.DMA((steps,)),
        ],
        compiler_params=params(),
        cost_estimate=cost(0, 0),
        name="local_back",
    )(me, count, rows, cols, places, *far_memory(grad, dgate, tiles, w_gate, back, *made))


def add_arrived(me, sums, arrived, rows, features, grad, w_value, w_gate, shifts, n, tile):
    steps, _, width = features.shape
    count = len(shifts)
    most = 3
    summed = True

    def body(me_ref, rows_in, f_ref, c_ref, wv_ref, wg_ref, *rest):
        parts, rest = rest[:count], rest[count:]
        if summed:
            s_ref, made_ref, sums_ref, s_buf, *rest = rest
        else:
            made_ref, *rest = rest
        p_buf, f_buf, c_buf, w_buf, made, sem, w_sem, made_sem, rows_ref, id_sem = rest
        ids = id_copies((rows_in,), (rows_ref,), id_sem)
        first = [pltpu.make_async_copy(ref, w_buf.at[i], w_sem.at[i]) for i, ref in enumerate((wg_ref, wv_ref))]
        first += [pltpu.make_async_copy(parts[j], p_buf.at[j], sem.at[0, j]) for j in range(count)]
        for load in first:
            load.start()
        ids[0].wait()
        then = []
        for j, shift in enumerate(shifts):
            at = pl.ds(pl.multiple_of(rows_ref[source_of(me_ref[0], shift, n)] * tile, tile), tile)
            then.append(pltpu.make_async_copy(f_ref.at[:, at, :], f_buf.at[j], sem.at[1, j]))
            then.append(pltpu.make_async_copy(c_ref.at[:, at, :], c_buf.at[j], sem.at[2, j]))
        for load in then:
            load.start()
        if summed:
            old = pltpu.make_async_copy(s_ref, s_buf, w_sem.at[2])
            old.start()
        for load in first:
            load.wait()
        stores = []
        for low in range(0, count, most):
            some = slice(low, min(low + most, count))
            for load in then[2 * some.start : 2 * some.stop]:
                load.wait()
            p, f, c = [flat_rows(buf[some]) for buf in (p_buf, f_buf, c_buf)]
            kept, dagg, dgate = gate_terms(f, c, p, w_buf[1], w_buf[0])
            shape = (some.stop - some.start, steps, tile, width)
            made[some, 0] = kept.astype(BF16).reshape(shape)
            made[some, 1] = mm_nt(dgate, w_buf[0]).astype(BF16).reshape(shape)
            store = pltpu.make_async_copy(made.at[some], made_ref.at[some], made_sem.at[low])
            store.start()
            stores.append(store)
            if summed and low == 0:
                old.wait()
                sums_ref[0] = s_buf[0] + mm_tn(p, dagg)
                sums_ref[1] = s_buf[1] + mm_tn(f, dgate)
            elif summed:
                sums_ref[0] += mm_tn(p, dagg)
                sums_ref[1] += mm_tn(f, dgate)
        for store in stores:
            store.wait()

    many = pltpu.VMEM((count, steps, tile, width), BF16)
    pair = (count, 2, steps, tile, width)
    operands = far_memory(rows, features, grad, w_value, w_gate) + list(arrived)
    out_shape, out_specs, scratch = [pltpu.HBM(pair, BF16)], [ANY], []
    if summed:
        operands += far_memory(sums)
        out_shape.append(pltpu.HBM(sums.shape, F32))
        out_specs.append(VMEM)
        scratch.append(pltpu.VMEM(sums.shape, F32))
    return pl.pallas_call(
        body,
        out_shape=out_shape,
        in_specs=[SMEM] + [ANY] * len(operands),
        out_specs=out_specs,
        scratch_shapes=scratch
        + [
            many,
            many,
            many,
            pltpu.VMEM((2, width, width), BF16),
            pltpu.VMEM(pair, BF16),
            pltpu.SemaphoreType.DMA((3, count)),
            pltpu.SemaphoreType.DMA((3,)),
            pltpu.SemaphoreType.DMA((count,)),
        ]
        + id_memory(n, 1),
        compiler_params=params(),
        cost_estimate=cost(0, 0),
        name="add_arrived" if summed else "arrived_terms",
    )(me, *operands)


def add_late(me, sums, arrived, rows, features, grad, w_value, w_gate, shifts, n, tile, place, level, wire):
    steps, _, width = features.shape
    count = len(shifts)
    size = level[2]
    lines = 2 * width // size

    def body(me_ref, place_ref, rows_in, f_ref, c_ref, wv_ref, wg_ref, s_ref, *rest):
        parts, (keep_ref, *send_refs), made_ref, rest = rest[:count], rest[count : count + size], rest[count + size], rest[count + size + 1 :]
        p_buf, f_buf, c_buf, w_buf, total, wired, made, sem, w_sem, done_sem, rows_ref, id_sem = rest
        ids = id_copies((rows_in,), (rows_ref,), id_sem)
        first = [pltpu.make_async_copy(ref, w_buf.at[i], w_sem.at[i]) for i, ref in enumerate((wg_ref, wv_ref))]
        first += [pltpu.make_async_copy(parts[j], p_buf.at[j], sem.at[0, j]) for j in range(count)]
        old = pltpu.make_async_copy(s_ref, total, w_sem.at[2])
        for load in first:
            load.start()
        ids[0].wait()
        then = []
        for j, shift in enumerate(shifts):
            at = pl.ds(pl.multiple_of(rows_ref[source_of(me_ref[0], shift, n)] * tile, tile), tile)
            then.append(pltpu.make_async_copy(f_ref.at[:, at, :], f_buf.at[j], sem.at[1, j]))
            then.append(pltpu.make_async_copy(c_ref.at[:, at, :], c_buf.at[j], sem.at[2, j]))
        for load in then:
            load.start()
        old.start()
        for load in first + then:
            load.wait()
        p, f, c = [flat_rows(buf[...]) for buf in (p_buf, f_buf, c_buf)]
        kept, dagg, dgate = gate_terms(f, c, p, w_buf[1], w_buf[0])
        value = mm_tn(p, dagg)
        gate = mm_tn(f, dgate)
        old.wait()
        total[:width, :] += value
        total[width:, :] += gate
        wired[...] = total[...].astype(wire)
        stores = []
        for i, (source, to) in enumerate([(total, keep_ref)] + [(wired, ref) for ref in send_refs]):
            mine = pl.ds(pl.multiple_of(lax.rem(place_ref[0] + i, size) * lines, lines), lines)
            stores.append(pltpu.make_async_copy(source.at[mine, :], to, done_sem.at[i]))
            stores[-1].start()
        shape = (count, steps, tile, width)
        made[:, 0] = kept.astype(BF16).reshape(shape)
        made[:, 1] = dgate.reshape(shape)
        stores.append(pltpu.make_async_copy(made, made_ref, done_sem.at[size]))
        stores[-1].start()
        for store in stores:
            store.wait()

    many = pltpu.VMEM((count, steps, tile, width), BF16)
    pair = (count, 2, steps, tile, width)
    return pl.pallas_call(
        body,
        out_shape=[pltpu.HBM((lines, width), F32)]
        + [pltpu.HBM((lines, width), wire)] * (size - 1)
        + [pltpu.HBM(pair, BF16)],
        in_specs=[SMEM, SMEM] + [ANY] * (6 + count),
        out_specs=[ANY] * (size + 1),
        scratch_shapes=[
            many,
            many,
            many,
            pltpu.VMEM((2, width, width), BF16),
            pltpu.VMEM((2 * width, width), F32),
            pltpu.VMEM((2 * width, width), wire),
            pltpu.VMEM(pair, BF16),
            pltpu.SemaphoreType.DMA((3, count)),
            pltpu.SemaphoreType.DMA((3,)),
            pltpu.SemaphoreType.DMA((size + 1,)),
        ]
        + id_memory(n, 1),
        compiler_params=params(),
        cost_estimate=cost(0, 0),
        name="add_late",
    )(me, place, *far_memory(rows, features, grad, w_value, w_gate, sums.reshape(2 * width, width)), *arrived)


def settle(me, kept, features, base, made, rows, groups, n, tile):
    steps, assets, width = kept.shape
    blocks = assets // tile
    per = 2 if blocks % 2 == 0 else 1
    sets = len(made)

    def body(me_ref, rows_ref, k_ref, f_ref, b_ref, *rest):
        parts, (out_ref, grads_ref, acc) = rest[:sets], rest[sets:]
        b = pl.program_id(0)
        grads_ref[...] = b_ref[...].astype(BF16)
        acc[...] = f_ref[...].astype(F32) + k_ref[...].astype(F32)
        for part, shifts in zip(parts, groups):
            for j, shift in enumerate(shifts):
                place = rows_ref[source_of(me_ref[0], shift, n)] - b * per

                @pl.when((place >= 0) & (place < per))
                def _():
                    acc[:, pl.ds(pl.multiple_of(place * tile, tile), tile), :] += part[j, 0].astype(F32)

        out_ref[...] = acc[...].astype(BF16)

    line = pl.BlockSpec((steps, per * tile, width), lambda b: (0, b, 0))
    pieces = [pl.BlockSpec((x.shape[0], 1) + x.shape[2:], lambda b: (0,) * 5) for x in made]
    return pl.pallas_call(
        body,
        grid=(blocks // per,),
        out_shape=[pltpu.HBM((steps, assets, width), BF16)] * 2,
        in_specs=[SMEM, SMEM, line, line, line] + pieces,
        out_specs=[line, line],
        scratch_shapes=[pltpu.VMEM((steps, per * tile, width), F32)],
        compiler_params=params(),
        cost_estimate=cost(0, 0),
        name="settle",
    )(me, rows, *far_memory(kept, features, base, *made))


def finish(step, grads, base, returned, cols, live, tiles, n):
    steps, assets, width = base.shape
    tile = tiles.shape[1]

    def body(cols_ref, live_ref, r_in, tiles_in, b_in, _, out_ref, r_ref, tiles_ref, b_ref, made, sem, b_sem, done_sem):
        others = [pltpu.make_async_copy(tiles_in, tiles_ref, sem.at[0]), pltpu.make_async_copy(r_in, r_ref, sem.at[1])]
        for load in others:
            load.start()
        places = [pl.ds(pl.multiple_of(cols_ref[of] * tile, tile), tile) for of in range(n)]
        blocks = [pltpu.make_async_copy(b_in.at[step, places[of], :], b_ref.at[of], b_sem.at[of]) for of in range(n)]
        for load in blocks:
            load.start()
        owner = []
        for of in range(n):
            first = jnp.int32(of)
            for other in reversed(range(of)):
                first = jnp.where(cols_ref[other] == cols_ref[of], other, first)
            owner.append(first)
        for load in others + blocks:
            load.wait()
        for of in range(n):
            used = tiles_ref[of] * live_ref[of].astype(F32).astype(BF16)
            b_ref[owner[of]] += mm_tn(used, r_ref[of])
        stores = [pltpu.make_async_copy(made.at[of], out_ref.at[step, places[of], :], done_sem.at[of]) for of in range(n)]
        for of in range(n):

            @pl.when(owner[of] == of)
            def _():
                made[of] = b_ref[of].astype(BF16)
                stores[of].start()

        for of in range(n):

            @pl.when(owner[of] == of)
            def _():
                stores[of].wait()

    block = pltpu.VMEM((n, tile, width), BF16)
    return pl.pallas_call(
        body,
        out_shape=pltpu.HBM(grads.shape, BF16),
        in_specs=[SMEM, SMEM] + [ANY] * 4,
        out_specs=ANY,
        scratch_shapes=[
            block,
            pltpu.VMEM(tiles.shape, BF16),
            pltpu.VMEM((n, tile, width), F32),
            block,
            pltpu.SemaphoreType.DMA((2,)),
            pltpu.SemaphoreType.DMA((n,)),
            pltpu.SemaphoreType.DMA((n,)),
        ],
        input_output_aliases={5: 0},
        compiler_params=params(),
        cost_estimate=cost(0, 0),
        name="finish",
    )(cols, live, returned, *far_memory(tiles, base, grads))


def levels(tm, asset):
    low = max(d for d in range(1, math.isqrt(asset) + 1) if asset % d == 0)
    pair = 2 if tm % 2 == 0 else 1
    return [("tm", 1, pair, tm), ("tm", pair, tm // pair, tm), ("asset", 1, low, asset), ("asset", low, asset // low, asset)]


def member(level):
    axis, stride, size, _ = level
    return (lax.axis_index(axis) // stride) % size


def pairs_of(level, shift):
    _, stride, size, n = level
    return [(i, i + ((i // stride + shift) % size - (i // stride) % size) * stride) for i in range(n)]


def scatter_sum(terms, level, wire):
    axis, _, size, _ = level
    me = member(level)

    def entry(index):
        return sum(lax.dynamic_index_in_dim(x, index, 0, keepdims=False) for x in terms)

    arrived = [lax.ppermute(entry((me + s) % size).astype(wire), axis, pairs_of(level, s)) for s in range(1, size)]
    total = entry(me)
    for part in arrived:
        total = total + part.astype(F32)
    return total


def butterfly_sum(x, level, wire):
    axis, _, size, _ = level
    if size & (size - 1):
        return lax.psum(x, axis, axis_index_groups=groups_of(level))
    shift = 1
    while shift < size:
        x = x.astype(wire)
        x = x.astype(F32) + lax.ppermute(x, axis, [(i, i ^ (shift * level[1])) for i in range(level[3])]).astype(F32)
        shift *= 2
    return x


def groups_of(level):
    _, stride, size, n = level
    return [[i + s * stride for s in range(size)] for i in range(n) if (i // stride) % size == 0]


def spread(x, level):
    axis, _, size, _ = level
    return [x] + [lax.ppermute(x, axis, pairs_of(level, s)) for s in range(1, size)]


def unshuffle(x, stacked, placed, shape):
    place = jnp.arange(math.prod(level[2] for level in placed), dtype=jnp.int32)
    digits, stride = {}, 1
    for level in reversed(placed):
        digits[level] = (place // stride) % level[2]
        stride *= level[2]
    index, stride = 0, 1
    for level in reversed(stacked):
        index = index + ((member(level) - digits[level]) % level[2]) * stride
        stride *= level[2]
    flat = x.reshape(place.shape[0], -1, shape[-1])
    return jnp.take(flat, index, axis=0, mode="clip").reshape(shape).astype(F32)


def per_device(
    features,
    w_value,
    w_gate,
    cotangent,
    local_rows,
    local_cols,
    local_count,
    local_tiles,
    remote_rows,
    remote_cols,
    remote_live,
    remote_tiles,
):
    steps, assets, width = features.shape
    tile = local_tiles.shape[1]
    n = lax.axis_size("asset")
    tm = lax.axis_size("tm")
    me = lax.axis_index("asset").astype(jnp.int32).reshape(1)
    flat = features.reshape(-1, width)
    grad = cotangent.reshape(-1, width)

    far = list(range(n // 2, n))[::-1]
    near = list(range(1, n // 2))
    shifts = far + near
    lead = max(1, len(far) - 1)
    first, second = far[:lead] + near[:2], far[lead:] + near[2:]
    late = far[-2:] + near[2:]
    early = [s for s in shifts if s not in late]
    weights = (w_value, w_gate)
    graph = (local_count, local_rows, local_cols, local_tiles)

    sent = dict(zip(shifts, send_forward(me, features, remote_tiles, remote_cols, remote_live, shifts, n)))
    came = {s: exchange(sent[s], s, n) for s in first}
    kept, dgate, back, sums, *owed = local_forward(*graph, features, cotangent, *weights, remote_rows)
    for s in second:
        came[s] = exchange(after(sent[s], sums, came[far[0]], came[near[0]]), s, n)
    made_early, sums = add_arrived(
        me, sums, [came[s] for s in early], remote_rows, features, cotangent, *weights, early, n, tile
    )
    pair, column, row, line = levels(tm, n)
    whole = ("tm", 1, tm, tm)
    place = member(whole).astype(jnp.int32).reshape(1)
    keep, *sends, made_late = add_late(
        me, sums, [came[s] for s in late], remote_rows, features, cotangent, *weights, late, n, tile, place, whole, BF16
    )

    def send_back(t, *before):
        return lax.all_to_all(after(owed[t], *before), "asset", 0, 0, tiled=True)

    returned = [send_back(t, made_early, *[came[s] for s in late]) for t in range(steps // 2)]
    made, groups = (made_early, made_late), (early, late)
    base = local_back(me, *graph, back, cotangent, dgate, made, remote_rows, groups, w_gate, n)
    output, grad_features = settle(me, kept, features, base, made, remote_rows, groups, n, tile)
    terms = [keep] + [lax.ppermute(x, "tm", pairs_of(whole, i + 1)) for i, x in enumerate(sends)]
    terms[1] = after(terms[1], base)
    shape = (row[2], keep.shape[0] // row[2], width)
    terms = [x.astype(F32).reshape(shape) for x in terms]
    sums = after(scatter_sum(terms, row, BF16), *returned)
    sums = butterfly_sum(sums, line, BF16).astype(BF16)
    returned += [send_back(t, sums) for t in range(steps // 2, steps)]

    def finish_step(t):
        return finish(t, grad_features, base, returned[t], remote_cols, remote_live, remote_tiles, n)

    for t in range(steps // 2):
        grad_features = finish_step(t)
    sums = jnp.stack(spread(sums, row))
    sums = jnp.stack(spread(sums, column))
    sums = after(sums, grad_features, output)
    sums = jnp.stack(spread(sums, pair))
    scale = float(steps * assets * tm * n) ** (-0.5)
    sums = unshuffle(sums, [pair, column, row], [column, pair, row], (2, width, width)) * scale
    for t in range(steps // 2, steps):
        grad_features = finish_step(t)
    return output, grad_features, sums[0], sums[1]


def solution(mesh):
    return jax.shard_map(
        per_device,
        mesh=mesh,
        in_specs=(
            P("tm", "asset", None),
            P(),
            P(),
            P("tm", "asset", None),
            P("asset"),
            P("asset"),
            P("asset"),
            P("asset", None, None),
            P("asset"),
            P("asset"),
            P("asset"),
            P("asset", None, None),
        ),
        out_specs=(P("tm", "asset", None), P("tm", "asset", None), P(), P()),
        check_vma=False,
    )
```

```python
import math

import jax
import jax.numpy as jnp
from jax import lax
from jax.experimental import pallas as pl
from jax.experimental.pallas import tpu as pltpu
from jax.sharding import PartitionSpec as P

F32 = jnp.float32
BF16 = jnp.bfloat16
ANY = pl.BlockSpec(memory_space=pl.ANY)
VMEM = pl.BlockSpec(memory_space=pltpu.VMEM)
SMEM = pl.BlockSpec(memory_space=pltpu.SMEM)
MIB = 1 << 20


def params(mib=40):
    return pltpu.CompilerParams(vmem_limit_bytes=mib * MIB)


def cost(flops, moved):
    return pl.CostEstimate(flops=int(flops), bytes_accessed=int(moved), transcendentals=0)


def mm(a, b):
    return lax.dot_general(a, b, (((1,), (0,)), ((), ())), preferred_element_type=F32)


def mm_tn(a, b):
    return lax.dot_general(a, b, (((0,), (0,)), ((), ())), preferred_element_type=F32)


def mm_nt(a, b):
    return lax.dot_general(a, b, (((1,), (1,)), ((), ())), preferred_element_type=F32)


def far_memory(*arrays):
    return [pltpu.with_memory_space_constraint(x, pltpu.HBM) for x in arrays]


def id_memory(n, count):
    return [pltpu.SMEM((n,), jnp.int32)] * count + [pltpu.SemaphoreType.DMA((count,))]


def id_copies(sources, buffers, sem):
    copies = [pltpu.make_async_copy(source, buffer, sem.at[i]) for i, (source, buffer) in enumerate(zip(sources, buffers))]
    for copy in copies:
        copy.start()
    return copies


def flat_rows(x):
    return x.reshape(-1, x.shape[-1])


def after(x, *others):
    return lax.optimization_barrier((x,) + others)[0]


def row_chunk(rows, most):
    return max(c for c in range(8, most + 1, 8) if rows % c == 0)


def target_of(index, shift, n):
    return index ^ shift if n & (n - 1) == 0 else (index + shift) % n


def source_of(index, shift, n):
    return index ^ shift if n & (n - 1) == 0 else (index + n - shift) % n


def exchange(block, shift, n):
    return lax.ppermute(block, "asset", [(i, target_of(i, shift, n)) for i in range(n)])


def send_forward(me, features, tiles, cols, live, shifts, n):
    steps, _, width = features.shape
    tile = tiles.shape[1]
    count = len(shifts)

    def body(me_ref, cols_in, live_in, tiles_ref, f_ref, *rest):
        outs, (weights, blocks, made, tile_sem, block_sem, made_sem) = rest[:count], rest[count : count + 6]
        cols_ref, live_ref, id_sem = rest[count + 6 :]
        ids = id_copies((cols_in, live_in), (cols_ref, live_ref), id_sem)
        loads = []
        for j, shift in enumerate(shifts):
            to = target_of(me_ref[0], shift, n)
            loads.append([pltpu.make_async_copy(tiles_ref.at[to], weights.at[j], tile_sem.at[j])])
            loads[j][0].start()
        for copy in ids:
            copy.wait()
        for j, shift in enumerate(shifts):
            start = pl.multiple_of(cols_ref[target_of(me_ref[0], shift, n)] * tile, tile)
            loads[j].append(pltpu.make_async_copy(f_ref.at[:, pl.ds(start, tile), :], blocks.at[j], block_sem.at[j]))
            loads[j][1].start()
        stores = []
        for j, shift in enumerate(shifts):
            to = target_of(me_ref[0], shift, n)
            for copy in loads[j]:
                copy.wait()
            used = weights[j] * live_ref[to].astype(F32).astype(BF16)
            for t in range(steps):
                made[j, t] = mm(used, blocks[j, t]).astype(BF16)
            store = pltpu.make_async_copy(made.at[j], outs[j], made_sem.at[j])
            store.start()
            stores.append(store)
        for store in stores:
            store.wait()

    block = pltpu.HBM((steps, tile, width), BF16)
    size = steps * tile * width
    many = pltpu.VMEM((count, steps, tile, width), BF16)
    sems = pltpu.SemaphoreType.DMA((count,))
    return pl.pallas_call(
        body,
        out_shape=[block] * count,
        in_specs=[SMEM, ANY, ANY, ANY, ANY],
        out_specs=[ANY] * count,
        scratch_shapes=[pltpu.VMEM((count, tile, tile), BF16), many, many, sems, sems, sems] + id_memory(n, 2),
        compiler_params=params(),
        cost_estimate=cost(2 * count * size * tile, 4 * count * size),
        name="send_forward",
    )(me, *far_memory(cols, live, tiles, features))


def place_tiles(dense, tiles_ref, count, rows_ref, cols_ref, turned):
    tile = tiles_ref.shape[1]
    dense[...] = jnp.zeros(dense.shape, BF16)

    @pl.loop(0, count)
    def _(l):
        row, col = (cols_ref[l], rows_ref[l]) if turned else (rows_ref[l], cols_ref[l])
        to = (pl.ds(pl.multiple_of(row * tile, tile), tile), pl.ds(pl.multiple_of(col * tile, tile), tile))
        new = tiles_ref[l].astype(F32)
        dense[to] = (dense[to].astype(F32) + (new.T if turned else new)).astype(BF16)


def gate_terms(f, c, g, wv, wg):
    gate = jax.nn.sigmoid(mm(f, wg))
    kept = gate * mm(g, wv)
    c = c.astype(F32)
    return kept, (c * gate).astype(BF16), (c * kept * (1.0 - gate)).astype(BF16)


def load_ids(sources, buffers, sem):
    for copy in id_copies(sources, buffers, sem):
        copy.wait()


def local_forward(count, rows, cols, tiles, features, grad, w_value, w_gate, wanted):
    steps, assets, width = features.shape
    tile = tiles.shape[1]
    n = wanted.shape[0]
    chunk = row_chunk(assets, 5 * tile)
    turns = assets // chunk

    def body(count_ref, rows_ref, cols_ref, wanted_ref, tiles_ref, c_ref, wv_ref, wg_ref, f_in, *rest):
        kept_ref, dgate_ref, back_ref, sums_ref = rest[:4]
        owed, (dense, f_ref, r_ref, sem, r_sem) = rest[4 : 4 + steps], rest[4 + steps :]
        t, i = pl.program_id(0), pl.program_id(1)
        loads = [pltpu.make_async_copy(f_in.at[s], f_ref.at[s], sem.at[s]) for s in range(steps)]

        @pl.when((t == 0) & (i == 0))
        def _():
            for load in loads:
                load.start()
            place_tiles(dense, tiles_ref, count_ref[0], rows_ref, cols_ref, False)
            sums_ref[...] = jnp.zeros(sums_ref.shape, F32)

        for s in range(steps):

            @pl.when((t == s) & (i == 0))
            def _():
                loads[s].wait()

        at = pl.ds(pl.multiple_of(i * chunk, chunk), chunk)
        f = f_ref[t, at, :]
        g = mm(dense[at, :], f_ref[t]).astype(BF16)
        kept, dagg, dgate = gate_terms(f, c_ref[0], g, wv_ref[...], wg_ref[...])
        back = mm_nt(dagg, wv_ref[...]).astype(BF16)
        back_ref[0] = back
        r_ref[at, :] = back
        kept_ref[0] = kept.astype(BF16)
        dgate_ref[0] = dgate
        sums_ref[0] += mm_tn(g, dagg)
        sums_ref[1] += mm_tn(f, dgate)

        @pl.when(i == turns - 1)
        def _():
            for s in range(steps):

                @pl.when(t == s)
                def _():
                    stores = []
                    for d in range(n):
                        block = pl.ds(pl.multiple_of(wanted_ref[d] * tile, tile), tile)
                        stores.append(pltpu.make_async_copy(r_ref.at[block, :], owed[s].at[d], r_sem.at[d]))
                    for store in stores:
                        store.start()
                    for store in stores:
                        store.wait()

    line = pl.BlockSpec((1, chunk, width), lambda t, i: (t, i, 0))
    weight = pl.BlockSpec((width, width), lambda t, i: (0, 0))
    return pl.pallas_call(
        body,
        grid=(steps, turns),
        out_shape=[pltpu.HBM(features.shape, BF16)] * 3
        + [pltpu.HBM((2, width, width), F32)]
        + [pltpu.HBM((n, tile, width), BF16)] * steps,
        in_specs=[SMEM] * 4 + [pl.BlockSpec(tiles.shape, lambda t, i: (0, 0, 0)), line, weight, weight, ANY],
        out_specs=[line, line, line, pl.BlockSpec((2, width, width), lambda t, i: (0, 0, 0))] + [ANY] * steps,
        scratch_shapes=[
            pltpu.VMEM((assets, assets), BF16),
            pltpu.VMEM(features.shape, BF16),
            pltpu.VMEM((assets, width), BF16),
            pltpu.SemaphoreType.DMA((steps,)),
            pltpu.SemaphoreType.DMA((n,)),
        ],
        compiler_params=params(),
        cost_estimate=cost(0, 0),
        name="local_forward",
    )(count, rows, cols, wanted, *far_memory(tiles, grad, w_value, w_gate, features))


def local_back(me, count, rows, cols, tiles, back, grad, dgate, made, places, groups, w_gate, n):
    steps, assets, width = back.shape
    tile = tiles.shape[1]
    chunk = row_chunk(assets, 5 * tile)
    per = chunk // tile
    shapes = [(x.shape[0],) + x.shape[2:] for x in made]

    def body(me_ref, count_ref, rows_ref, cols_ref, places_ref, c_ref, d_ref, tiles_in, w_in, r_in, early_in, late_in, *rest):
        out_ref, dense, tiles_ref, w_ref, r_ref, early_ref, late_ref, turned, sem, r_sem = rest
        t, i = pl.program_id(0), pl.program_id(1)
        loads = [pltpu.make_async_copy(r_in.at[s], r_ref.at[s], r_sem.at[s]) for s in range(steps)]
        sides = ((tiles_in, tiles_ref), (w_in, w_ref), (late_in.at[:, 1], late_ref), (early_in.at[:, 1], early_ref))
        others = [pltpu.make_async_copy(source, to, sem.at[k]) for k, (source, to) in enumerate(sides)]

        @pl.when((t == 0) & (i == 0))
        def _():
            for load in others[:1] + loads[:1] + others[1:] + loads[1:]:
                load.start()
            others[0].wait()
            place_tiles(dense, tiles_ref, count_ref[0], rows_ref, cols_ref, True)
            for load in others[1:]:
                load.wait()
            turned[...] = mm_nt(flat_rows(late_ref[...]), w_ref[...]).reshape(turned.shape)

        for s in range(steps):

            @pl.when((t == s) & (i == 0))
            def _():
                loads[s].wait()

        at = pl.ds(pl.multiple_of(i * chunk, chunk), chunk)
        out_ref[0] = c_ref[0].astype(F32) + mm(dense[at, :], r_ref[t]) + mm_nt(d_ref[0], w_ref[...])
        for part, shifts in zip((early_ref, turned), groups):
            for j, shift in enumerate(shifts):
                place = places_ref[source_of(me_ref[0], shift, n)] - i * per

                @pl.when((place >= 0) & (place < per))
                def _():
                    out_ref[0, pl.ds(pl.multiple_of(place * tile, tile), tile), :] += part[j, t].astype(F32)

    line = pl.BlockSpec((1, chunk, width), lambda t, i: (t, i, 0))
    return pl.pallas_call(
        body,
        grid=(steps, assets // chunk),
        out_shape=pltpu.HBM(back.shape, F32),
        in_specs=[SMEM] * 5 + [line, line] + [ANY] * 5,
        out_specs=line,
        scratch_shapes=[
            pltpu.VMEM((assets, assets), BF16),
            pltpu.VMEM(tiles.shape, BF16),
            pltpu.VMEM(w_gate.shape, BF16),
            pltpu.VMEM(back.shape, BF16),
            pltpu.VMEM(shapes[0], BF16),
            pltpu.VMEM(shapes[1], BF16),
            pltpu.VMEM(shapes[1], F32),
            pltpu.SemaphoreType.DMA((4,)),
            pltpu.SemaphoreType.DMA((steps,)),
        ],
        compiler_params=params(),
        cost_estimate=cost(0, 0),
        name="local_back",
    )(me, count, rows, cols, places, *far_memory(grad, dgate, tiles, w_gate, back, *made))


def add_arrived(me, sums, arrived, rows, features, grad, w_value, w_gate, shifts, n, tile):
    steps, _, width = features.shape
    count = len(shifts)
    most = 3
    summed = True

    def body(me_ref, rows_in, f_ref, c_ref, wv_ref, wg_ref, *rest):
        parts, rest = rest[:count], rest[count:]
        if summed:
            s_ref, made_ref, sums_ref, s_buf, *rest = rest
        else:
            made_ref, *rest = rest
        p_buf, f_buf, c_buf, w_buf, made, sem, w_sem, made_sem, rows_ref, id_sem = rest
        ids = id_copies((rows_in,), (rows_ref,), id_sem)
        first = [pltpu.make_async_copy(ref, w_buf.at[i], w_sem.at[i]) for i, ref in enumerate((wg_ref, wv_ref))]
        first += [pltpu.make_async_copy(parts[j], p_buf.at[j], sem.at[0, j]) for j in range(count)]
        for load in first:
            load.start()
        ids[0].wait()
        then = []
        for j, shift in enumerate(shifts):
            at = pl.ds(pl.multiple_of(rows_ref[source_of(me_ref[0], shift, n)] * tile, tile), tile)
            then.append(pltpu.make_async_copy(f_ref.at[:, at, :], f_buf.at[j], sem.at[1, j]))
            then.append(pltpu.make_async_copy(c_ref.at[:, at, :], c_buf.at[j], sem.at[2, j]))
        for load in then:
            load.start()
        if summed:
            old = pltpu.make_async_copy(s_ref, s_buf, w_sem.at[2])
            old.start()
        for load in first:
            load.wait()
        stores = []
        for low in range(0, count, most):
            some = slice(low, min(low + most, count))
            for load in then[2 * some.start : 2 * some.stop]:
                load.wait()
            p, f, c = [flat_rows(buf[some]) for buf in (p_buf, f_buf, c_buf)]
            kept, dagg, dgate = gate_terms(f, c, p, w_buf[1], w_buf[0])
            shape = (some.stop - some.start, steps, tile, width)
            made[some, 0] = kept.astype(BF16).reshape(shape)
            made[some, 1] = mm_nt(dgate, w_buf[0]).astype(BF16).reshape(shape)
            store = pltpu.make_async_copy(made.at[some], made_ref.at[some], made_sem.at[low])
            store.start()
            stores.append(store)
            if summed and low == 0:
                old.wait()
                sums_ref[0] = s_buf[0] + mm_tn(p, dagg)
                sums_ref[1] = s_buf[1] + mm_tn(f, dgate)
            elif summed:
                sums_ref[0] += mm_tn(p, dagg)
                sums_ref[1] += mm_tn(f, dgate)
        for store in stores:
            store.wait()

    many = pltpu.VMEM((count, steps, tile, width), BF16)
    pair = (count, 2, steps, tile, width)
    operands = far_memory(rows, features, grad, w_value, w_gate) + list(arrived)
    out_shape, out_specs, scratch = [pltpu.HBM(pair, BF16)], [ANY], []
    if summed:
        operands += far_memory(sums)
        out_shape.append(pltpu.HBM(sums.shape, F32))
        out_specs.append(VMEM)
        scratch.append(pltpu.VMEM(sums.shape, F32))
    return pl.pallas_call(
        body,
        out_shape=out_shape,
        in_specs=[SMEM] + [ANY] * len(operands),
        out_specs=out_specs,
        scratch_shapes=scratch
        + [
            many,
            many,
            many,
            pltpu.VMEM((2, width, width), BF16),
            pltpu.VMEM(pair, BF16),
            pltpu.SemaphoreType.DMA((3, count)),
            pltpu.SemaphoreType.DMA((3,)),
            pltpu.SemaphoreType.DMA((count,)),
        ]
        + id_memory(n, 1),
        compiler_params=params(),
        cost_estimate=cost(0, 0),
        name="add_arrived" if summed else "arrived_terms",
    )(me, *operands)


def add_late(me, sums, arrived, rows, features, grad, w_value, w_gate, shifts, n, tile, place, level, wire):
    steps, _, width = features.shape
    count = len(shifts)
    size = level[2]
    lines = 2 * width // size

    def body(me_ref, place_ref, rows_in, f_ref, c_ref, wv_ref, wg_ref, s_ref, *rest):
        parts, (keep_ref, *send_refs), made_ref, rest = rest[:count], rest[count : count + size], rest[count + size], rest[count + size + 1 :]
        p_buf, f_buf, c_buf, w_buf, total, wired, made, sem, w_sem, done_sem, rows_ref, id_sem = rest
        ids = id_copies((rows_in,), (rows_ref,), id_sem)
        first = [pltpu.make_async_copy(ref, w_buf.at[i], w_sem.at[i]) for i, ref in enumerate((wg_ref, wv_ref))]
        first += [pltpu.make_async_copy(parts[j], p_buf.at[j], sem.at[0, j]) for j in range(count)]
        old = pltpu.make_async_copy(s_ref, total, w_sem.at[2])
        for load in first:
            load.start()
        ids[0].wait()
        then = []
        for j, shift in enumerate(shifts):
            at = pl.ds(pl.multiple_of(rows_ref[source_of(me_ref[0], shift, n)] * tile, tile), tile)
            then.append(pltpu.make_async_copy(f_ref.at[:, at, :], f_buf.at[j], sem.at[1, j]))
            then.append(pltpu.make_async_copy(c_ref.at[:, at, :], c_buf.at[j], sem.at[2, j]))
        for load in then:
            load.start()
        old.start()
        for load in first + then:
            load.wait()
        p, f, c = [flat_rows(buf[...]) for buf in (p_buf, f_buf, c_buf)]
        kept, dagg, dgate = gate_terms(f, c, p, w_buf[1], w_buf[0])
        value = mm_tn(p, dagg)
        gate = mm_tn(f, dgate)
        old.wait()
        total[:width, :] += value
        total[width:, :] += gate
        wired[...] = total[...].astype(wire)
        stores = []
        for i, (source, to) in enumerate([(total, keep_ref)] + [(wired, ref) for ref in send_refs]):
            mine = pl.ds(pl.multiple_of(lax.rem(place_ref[0] + i, size) * lines, lines), lines)
            stores.append(pltpu.make_async_copy(source.at[mine, :], to, done_sem.at[i]))
            stores[-1].start()
        shape = (count, steps, tile, width)
        made[:, 0] = kept.astype(BF16).reshape(shape)
        made[:, 1] = dgate.reshape(shape)
        stores.append(pltpu.make_async_copy(made, made_ref, done_sem.at[size]))
        stores[-1].start()
        for store in stores:
            store.wait()

    many = pltpu.VMEM((count, steps, tile, width), BF16)
    pair = (count, 2, steps, tile, width)
    return pl.pallas_call(
        body,
        out_shape=[pltpu.HBM((lines, width), F32)]
        + [pltpu.HBM((lines, width), wire)] * (size - 1)
        + [pltpu.HBM(pair, BF16)],
        in_specs=[SMEM, SMEM] + [ANY] * (6 + count),
        out_specs=[ANY] * (size + 1),
        scratch_shapes=[
            many,
            many,
            many,
            pltpu.VMEM((2, width, width), BF16),
            pltpu.VMEM((2 * width, width), F32),
            pltpu.VMEM((2 * width, width), wire),
            pltpu.VMEM(pair, BF16),
            pltpu.SemaphoreType.DMA((3, count)),
            pltpu.SemaphoreType.DMA((3,)),
            pltpu.SemaphoreType.DMA((size + 1,)),
        ]
        + id_memory(n, 1),
        compiler_params=params(),
        cost_estimate=cost(0, 0),
        name="add_late",
    )(me, place, *far_memory(rows, features, grad, w_value, w_gate, sums.reshape(2 * width, width)), *arrived)


def settle(me, kept, features, base, made, rows, groups, n, tile):
    steps, assets, width = kept.shape
    blocks = assets // tile
    per = 2 if blocks % 2 == 0 else 1
    sets = len(made)

    def body(me_ref, rows_ref, k_ref, f_ref, b_ref, *rest):
        parts, (out_ref, grads_ref, acc) = rest[:sets], rest[sets:]
        b = pl.program_id(0)
        grads_ref[...] = b_ref[...].astype(BF16)
        acc[...] = f_ref[...].astype(F32) + k_ref[...].astype(F32)
        for part, shifts in zip(parts, groups):
            for j, shift in enumerate(shifts):
                place = rows_ref[source_of(me_ref[0], shift, n)] - b * per

                @pl.when((place >= 0) & (place < per))
                def _():
                    acc[:, pl.ds(pl.multiple_of(place * tile, tile), tile), :] += part[j, 0].astype(F32)

        out_ref[...] = acc[...].astype(BF16)

    line = pl.BlockSpec((steps, per * tile, width), lambda b: (0, b, 0))
    pieces = [pl.BlockSpec((x.shape[0], 1) + x.shape[2:], lambda b: (0,) * 5) for x in made]
    return pl.pallas_call(
        body,
        grid=(blocks // per,),
        out_shape=[pltpu.HBM((steps, assets, width), BF16)] * 2,
        in_specs=[SMEM, SMEM, line, line, line] + pieces,
        out_specs=[line, line],
        scratch_shapes=[pltpu.VMEM((steps, per * tile, width), F32)],
        compiler_params=params(),
        cost_estimate=cost(0, 0),
        name="settle",
    )(me, rows, *far_memory(kept, features, base, *made))


def finish(step, grads, base, returned, cols, live, tiles, n):
    steps, assets, width = base.shape
    tile = tiles.shape[1]

    def body(cols_ref, live_ref, r_in, tiles_in, b_in, _, out_ref, r_ref, tiles_ref, b_ref, made, sem, b_sem, done_sem):
        others = [pltpu.make_async_copy(tiles_in, tiles_ref, sem.at[0]), pltpu.make_async_copy(r_in, r_ref, sem.at[1])]
        for load in others:
            load.start()
        places = [pl.ds(pl.multiple_of(cols_ref[of] * tile, tile), tile) for of in range(n)]
        blocks = [pltpu.make_async_copy(b_in.at[step, places[of], :], b_ref.at[of], b_sem.at[of]) for of in range(n)]
        for load in blocks:
            load.start()
        owner = []
        for of in range(n):
            first = jnp.int32(of)
            for other in reversed(range(of)):
                first = jnp.where(cols_ref[other] == cols_ref[of], other, first)
            owner.append(first)
        for load in others:
            load.wait()
        for of in range(n):
            blocks[of].wait()
            used = tiles_ref[of] * live_ref[of].astype(F32).astype(BF16)
            b_ref[owner[of]] += mm_tn(used, r_ref[of])
        stores = [pltpu.make_async_copy(made.at[of], out_ref.at[step, places[of], :], done_sem.at[of]) for of in range(n)]
        for of in range(n):

            @pl.when(owner[of] == of)
            def _():
                made[of] = b_ref[of].astype(BF16)
                stores[of].start()

        for of in range(n):

            @pl.when(owner[of] == of)
            def _():
                stores[of].wait()

    block = pltpu.VMEM((n, tile, width), BF16)
    return pl.pallas_call(
        body,
        out_shape=pltpu.HBM(grads.shape, BF16),
        in_specs=[SMEM, SMEM] + [ANY] * 4,
        out_specs=ANY,
        scratch_shapes=[
            block,
            pltpu.VMEM(tiles.shape, BF16),
            pltpu.VMEM((n, tile, width), F32),
            block,
            pltpu.SemaphoreType.DMA((2,)),
            pltpu.SemaphoreType.DMA((n,)),
            pltpu.SemaphoreType.DMA((n,)),
        ],
        input_output_aliases={5: 0},
        compiler_params=params(),
        cost_estimate=cost(0, 0),
        name="finish",
    )(cols, live, returned, *far_memory(tiles, base, grads))


def levels(tm, asset):
    low = max(d for d in range(1, math.isqrt(asset) + 1) if asset % d == 0)
    pair = 2 if tm % 2 == 0 else 1
    return [("tm", 1, pair, tm), ("tm", pair, tm // pair, tm), ("asset", 1, low, asset), ("asset", low, asset // low, asset)]


def member(level):
    axis, stride, size, _ = level
    return (lax.axis_index(axis) // stride) % size


def pairs_of(level, shift):
    _, stride, size, n = level
    return [(i, i + ((i // stride + shift) % size - (i // stride) % size) * stride) for i in range(n)]


def scatter_sum(terms, level, wire):
    axis, _, size, _ = level
    me = member(level)

    def entry(index):
        return sum(lax.dynamic_index_in_dim(x, index, 0, keepdims=False) for x in terms)

    arrived = [lax.ppermute(entry((me + s) % size).astype(wire), axis, pairs_of(level, s)) for s in range(1, size)]
    total = entry(me)
    for part in arrived:
        total = total + part.astype(F32)
    return total


def butterfly_sum(x, level, wire):
    axis, _, size, _ = level
    if size & (size - 1):
        return lax.psum(x, axis, axis_index_groups=groups_of(level))
    shift = 1
    while shift < size:
        x = x.astype(wire)
        x = x.astype(F32) + lax.ppermute(x, axis, [(i, i ^ (shift * level[1])) for i in range(level[3])]).astype(F32)
        shift *= 2
    return x


def groups_of(level):
    _, stride, size, n = level
    return [[i + s * stride for s in range(size)] for i in range(n) if (i // stride) % size == 0]


def spread(x, level):
    axis, _, size, _ = level
    return [x] + [lax.ppermute(x, axis, pairs_of(level, s)) for s in range(1, size)]


def unshuffle(x, stacked, placed, shape):
    place = jnp.arange(math.prod(level[2] for level in placed), dtype=jnp.int32)
    digits, stride = {}, 1
    for level in reversed(placed):
        digits[level] = (place // stride) % level[2]
        stride *= level[2]
    index, stride = 0, 1
    for level in reversed(stacked):
        index = index + ((member(level) - digits[level]) % level[2]) * stride
        stride *= level[2]
    flat = x.reshape(place.shape[0], -1, shape[-1])
    return jnp.take(flat, index, axis=0, mode="clip").reshape(shape).astype(F32)


def per_device(
    features,
    w_value,
    w_gate,
    cotangent,
    local_rows,
    local_cols,
    local_count,
    local_tiles,
    remote_rows,
    remote_cols,
    remote_live,
    remote_tiles,
):
    steps, assets, width = features.shape
    tile = local_tiles.shape[1]
    n = lax.axis_size("asset")
    tm = lax.axis_size("tm")
    me = lax.axis_index("asset").astype(jnp.int32).reshape(1)
    flat = features.reshape(-1, width)
    grad = cotangent.reshape(-1, width)

    far = list(range(n // 2, n))[::-1]
    near = list(range(1, n // 2))
    shifts = far + near
    lead = max(1, len(far) - 1)
    first, second = far[:lead] + near[:2], far[lead:] + near[2:]
    late = far[-2:] + near[2:]
    early = [s for s in shifts if s not in late]
    weights = (w_value, w_gate)
    graph = (local_count, local_rows, local_cols, local_tiles)

    sent = dict(zip(shifts, send_forward(me, features, remote_tiles, remote_cols, remote_live, shifts, n)))
    came = {s: exchange(sent[s], s, n) for s in first}
    kept, dgate, back, sums, *owed = local_forward(*graph, features, cotangent, *weights, remote_rows)
    for s in second:
        came[s] = exchange(after(sent[s], sums, came[far[0]], came[near[0]]), s, n)
    made_early, sums = add_arrived(
        me, sums, [came[s] for s in early], remote_rows, features, cotangent, *weights, early, n, tile
    )
    pair, column, row, line = levels(tm, n)
    whole = ("tm", 1, tm, tm)
    place = member(whole).astype(jnp.int32).reshape(1)
    keep, *sends, made_late = add_late(
        me, sums, [came[s] for s in late], remote_rows, features, cotangent, *weights, late, n, tile, place, whole, BF16
    )

    def send_back(t, *before):
        return lax.all_to_all(after(owed[t], *before), "asset", 0, 0, tiled=True)

    returned = [send_back(t, made_early, *[came[s] for s in late]) for t in range(steps // 2)]
    made, groups = (made_early, made_late), (early, late)
    base = local_back(me, *graph, back, cotangent, dgate, made, remote_rows, groups, w_gate, n)
    output, grad_features = settle(me, kept, features, base, made, remote_rows, groups, n, tile)
    terms = [keep] + [lax.ppermute(x, "tm", pairs_of(whole, i + 1)) for i, x in enumerate(sends)]
    terms[1] = after(terms[1], base)
    shape = (row[2], keep.shape[0] // row[2], width)
    terms = [x.astype(F32).reshape(shape) for x in terms]
    sums = after(scatter_sum(terms, row, BF16), *returned)
    sums = butterfly_sum(sums, line, BF16).astype(BF16)
    returned += [send_back(t, sums) for t in range(steps // 2, steps)]

    def finish_step(t):
        return finish(t, grad_features, base, returned[t], remote_cols, remote_live, remote_tiles, n)

    for t in range(steps // 2):
        grad_features = finish_step(t)
    sums = jnp.stack(spread(sums, row))
    sums = jnp.stack(spread(sums, column))
    sums = after(sums, grad_features, output)
    sums = jnp.stack(spread(sums, pair))
    scale = float(steps * assets * tm * n) ** (-0.5)
    sums = unshuffle(sums, [pair, column, row], [column, pair, row], (2, width, width)) * scale
    for t in range(steps // 2, steps):
        grad_features = finish_step(t)
    return output, grad_features, sums[0], sums[1]


def solution(mesh):
    return jax.shard_map(
        per_device,
        mesh=mesh,
        in_specs=(
            P("tm", "asset", None),
            P(),
            P(),
            P("tm", "asset", None),
            P("asset"),
            P("asset"),
            P("asset"),
            P("asset", None, None),
            P("asset"),
            P("asset"),
            P("asset"),
            P("asset", None, None),
        ),
        out_specs=(P("tm", "asset", None), P("tm", "asset", None), P(), P()),
        check_vma=False,
    )
```
